256 devices in a mesh: role: 2 (over y_lo), grp: 32 (over z, x), tp: 4 (over y_hi, core).
Axes of the slice: x: 4, y: 4 (y_hi: 2, y_lo: 2; y = y_hi * 2 + y_lo), z: 8, core: 2. Of those that a mesh axis runs over, the one named last changes fastest.
Arguments:
- hidden_in: bfloat16 [8192, 4096], P(('role', 'grp')), may hold values from -20 to 20
- moe_gain: bfloat16 [4096], replicated, may hold values from 0.25 to 1.75
- router: bfloat16 [4096, 16], replicated, may hold values from -0.09375 to 0.09375
- routes: int32 [8192, 2], P(('role', 'grp')), may hold values from 0 to 15, all different within a row; in each aligned block of 128 rows (0 to 127, 128 to 255, ...) at most 24 rows name the same one
- gate_weight: bfloat16 [32, 4096, 768], P('grp', None, 'tp'), may hold values from -0.09375 to 0.09375
- up_weight: bfloat16 [32, 4096, 768], P('grp', None, 'tp'), may hold values from -0.09375 to 0.09375
- down_weight: bfloat16 [32, 768, 4096], P('grp', 'tp'), may hold values from -0.15625 to 0.15625
- attn_gain: bfloat16 [4096], replicated, may hold values from 0.25 to 1.75
- kv_weight: bfloat16 [4096, 2, 512], P(None, None, 'tp'), may hold values from -0.09375 to 0.09375
- queries: bfloat16 [8192, 8192], P(('role', 'grp'), 'tp'), may hold values from -8 to 8
- decode_cache: bfloat16 [1024, 4, 2, 128, 128], P(('role', 'grp'), 'tp'), may hold values from -8 to 8
- prompt_cache: bfloat16 [2048, 4, 2, 128, 128], P(('role', 'grp'), 'tp'), may hold values from -8 to 8
- handoff: int32 [64, 32], P(('role', 'grp')), may hold values from 0 to 31, each once within a row
- block_table: int32 [2048, 4], P(('role', 'grp')), may hold values from 0 to 47, as said below
- lengths: int32 [2048], P(('role', 'grp')), may hold values from 1 to 512
Outputs:
- residual_out: float32 [8192, 4096], P(('role', 'grp'), 'tp')
- new_kv: bfloat16 [8192, 2, 512], P(('role', 'grp'), None, 'tp')
- attn_out: bfloat16 [8192, 8192], P(('role', 'grp'), 'tp')
The draws below stay inside these ranges and needn't reach their ends.
Inputs may be any that keep to these rules, and one draw needn't show every extreme that they name: `routes`: a token's 2 experts differ; in the 128 tokens of one group at most 24 choose the same expert. `handoff`: each row names every prompt block of its prefill group once. `block_table`: the 4 entries of a row differ.
All inputs are finite; a program needn't handle non-finite values.
Results may differ from the reference program's by a relative error of at most 0.014.
Values may be sent and summed in bfloat16 or wider, within the bound.
No kernel may reach another device: no remote copies, remote signals or barrier semaphores. Data moves between devices by JAX's collectives and lax.ppermute only.
A program may use at most 128 MiB of HBM per device.

```python
import math
import jax
import jax.numpy as jnp
import numpy as np
from jax import lax

D = 4096
HEADS = 64
KV_HEADS = 4
HEAD_DIM = 128
MOE_FF = 1536
BLOCK = 128
MAX_BLOCKS = 4
DRAFT = 4
TOP = 2
REQ = 32
RES_BLOCKS = 16
GROUPS = 64
PEERS = 32
EXPERTS = 16
ROWS = 128
TOKENS = 8192
CAP = 24
UNITS = 192
LOCAL = 48


def draw_hidden_in(key, part):
    key = jax.random.fold_in(key, 1)
    key_one, key_two, key_three = jax.random.split(key, 3)
    col_scale = jnp.exp(jax.random.uniform(key_one, (1, D), minval=jnp.log(0.3), maxval=jnp.log(3.0)))
    row_scale = jnp.exp(jax.random.uniform(key_two, (TOKENS, 1), minval=jnp.log(0.5), maxval=jnp.log(1.5)))
    base_vals = jnp.clip(jax.random.normal(key_three, (TOKENS, D)), -4.0, 4.0)
    return (base_vals * col_scale * row_scale).astype(jnp.bfloat16)


def draw_router(key, part):
    key = jax.random.fold_in(key, 2)
    key_one = jax.random.fold_in(key, 0)
    return (jnp.clip(jax.random.normal(key_one, (D, EXPERTS)), -4.0, 4.0) / D ** 0.5).astype(jnp.bfloat16)


def draw_queries(key, part):
    key = jax.random.fold_in(key, 3)
    key_one = jax.random.fold_in(key, 0)
    base_vals = jnp.clip(jax.random.normal(key_one, (TOKENS, HEADS, HEAD_DIM)), -6.0, 6.0)
    return base_vals.reshape(TOKENS, HEADS * HEAD_DIM).astype(jnp.bfloat16)


def draw_decode_cache(key, part):
    key = jax.random.fold_in(key, 4)
    dims_all = (GROUPS * RES_BLOCKS, KV_HEADS, 2, BLOCK, HEAD_DIM)
    return jnp.clip(jax.random.normal(key, dims_all), -6.0, 6.0).astype(jnp.bfloat16)


def draw_prompt_cache(key, part):
    key = jax.random.fold_in(key, 5)
    dims_all = (GROUPS * PEERS, KV_HEADS, 2, BLOCK, HEAD_DIM)
    return jnp.clip(jax.random.normal(key, dims_all), -6.0, 6.0).astype(jnp.bfloat16)


def draw_block_table(key, part):
    key = jax.random.fold_in(key, 6)
    scores = jax.random.randint(key, (GROUPS * REQ, LOCAL), 0, 1 << 20) * LOCAL + jnp.arange(LOCAL, dtype=jnp.int32)[None, :]
    ranked = jnp.argsort(scores, axis=1)
    return ranked[:, :MAX_BLOCKS].astype(jnp.int32)


def draw_lengths(key, part):
    key = jax.random.fold_in(key, 7)
    key_one, key_two = jax.random.split(key, 2)
    total_rows = GROUPS * REQ
    longest = MAX_BLOCKS * BLOCK
    drawn = jax.random.randint(key_one, (total_rows,), 1, longest + 1)
    spot_idx = jax.random.randint(key_two, (), 0, total_rows)
    return jnp.where(jnp.arange(total_rows, dtype=jnp.int32) == spot_idx, longest, drawn).astype(jnp.int32)


def block_scale(stream_key, extent, cuts, smallest, top_value):
    gain, own = 1.0, jax.random.fold_in(stream_key, 6)
    for position, parts in cuts:
        heights = jnp.exp(jax.random.uniform(jax.random.fold_in(own, position), (parts,), jnp.float32, smallest / len(cuts), top_value / len(cuts)))
        gain = gain * jnp.repeat(heights, extent[position] // parts).reshape([-1 if axis == position else 1 for axis in range(len(extent))])
    return gain


def assign_block(stream_key, own, number, rows, count, top, most, lean):
    order = jax.random.permutation(stream_key, count)
    crowded, ordinary = shares(count, rows * top, most, lean, True), shares(count, rows * top, most, lean, False)
    places = jnp.arange(count)

    def named(tallies, rotation):
        used = int((tallies > 0).sum())
        fixed = max(1, used // 4)
        shifted = fixed + (places - fixed + rotation * (used - fixed)) % max(1, count - fixed)
        return jnp.zeros((count,), jnp.int32).at[order[jnp.where(places < fixed, places, shifted)]].set(jnp.asarray(tallies, jnp.int32))

    tallies = jnp.where(number % 4 == 0, named(crowded, number // 4), named(ordinary, number - number // 4 - 1))
    mixed = jax.random.permutation(jax.random.fold_in(own, 3), count)
    giver, taker = mixed[0:count // 2 * 2:2], mixed[1:count // 2 * 2:2]
    slack = jnp.minimum(tallies[giver] - 1, most - tallies[taker]) // 2
    slack = jnp.where((giver == order[0]) | (taker == order[0]) | (tallies[taker] == 0), 0, jnp.maximum(slack, 0))
    shifted = jax.random.randint(jax.random.fold_in(own, 4), (count // 2,), 0, 1 << 20) % (slack + 1)
    tallies = tallies.at[giver].add(-shifted).at[taker].add(shifted)
    members = jnp.searchsorted(jnp.cumsum(tallies), jnp.arange(rows * top), side="right").astype(jnp.int32)
    grid = members.reshape(top, rows).T
    grid = grid[jax.random.permutation(jax.random.fold_in(own, 1), rows)]
    rotation = jax.random.randint(jax.random.fold_in(own, 2), (rows, 1), 0, top)
    return jnp.take_along_axis(grid, (jnp.arange(top)[None, :] + rotation) % top, axis=1)


def shares(amount, total, most, lean, full):
    loads = [(1 << 20) // math.isqrt(standing ** lean) + 1 for standing in range(1, amount + 1)]
    largest = most if full else min(most, max(-(-total // amount), total * loads[0] // sum(loads)))
    least = 1 if total - largest >= amount - 1 else 0
    holding, rest = [largest] + [least] * (amount - 1), total - largest - least * (amount - 1)
    while rest > 0:
        free = [i for i in range(1, amount) if holding[i] < largest] or [i for i in range(1, amount) if holding[i] < most]
        pool, left = sum([loads[i] for i in free]), rest
        for i in free:
            more = min(most - holding[i], max(1, left * loads[i] // pool), rest)
            holding[i] = holding[i] + more
            rest = rest - more
    return np.array(holding)


def centred(rng, extent, scale, limit, cuts=(), kind=jnp.bfloat16):
    level = block_scale(rng, extent, cuts, -0.22, 0.18) if cuts else 1.0
    result = jax.random.normal(rng, extent, jnp.float32) * scale * level
    return jnp.minimum(jnp.maximum(result, -limit), limit).astype(kind)


def setup_inputs(seed: int = 0) -> dict:
    key_of = jax.random.split(jax.random.key(seed), 16)
    hidden_in = draw_hidden_in(jax.random.fold_in(key_of[15], 71), 0)
    moe_gain = jnp.clip(1.0 + 0.15 * jax.random.normal(key_of[1], (D,), jnp.float32), 0.25, 1.75).astype(jnp.bfloat16)
    router = draw_router(jax.random.fold_in(key_of[15], 71), 0)
    routes_keys = jax.random.split(jax.random.fold_in(key_of[3], 1), TOKENS // ROWS)
    routes_turns = jax.random.permutation(jax.random.fold_in(key_of[3], 3), TOKENS // ROWS)
    routes = jax.vmap(lambda own, number: assign_block(jax.random.fold_in(key_of[3], 2), own, number, ROWS, EXPERTS, TOP, CAP, 2))(routes_keys, routes_turns).reshape((TOKENS, TOP))
    gate_weight = centred(key_of[4], (2 * EXPERTS, D, MOE_FF // 2), D ** -0.5, 0.09375, ((0, 32), (2, 4)))
    up_weight = centred(key_of[5], (2 * EXPERTS, D, MOE_FF // 2), D ** -0.5, 0.09375, ((0, 32), (2, 4)))
    down_weight = centred(key_of[6], (2 * EXPERTS, MOE_FF // 2, D), MOE_FF ** -0.5, 0.15625, ((0, 32), (1, 4)))
    attn_gain = jnp.clip(1.0 + 0.15 * jax.random.normal(key_of[7], (D,), jnp.float32), 0.25, 1.75).astype(jnp.bfloat16)
    kv_weight = centred(key_of[8], (D, 2, KV_HEADS * HEAD_DIM), D ** -0.5, 0.09375, ((2, 4),))
    queries = draw_queries(jax.random.fold_in(key_of[15], 71), 0)
    decode_cache = draw_decode_cache(jax.random.fold_in(key_of[15], 71), 0)
    prompt_cache = draw_prompt_cache(jax.random.fold_in(key_of[15], 71), 0)
    handoff = jax.vmap(lambda own: jax.random.permutation(own, PEERS))(jax.random.split(key_of[12], GROUPS)).reshape((GROUPS, PEERS)).astype(jnp.int32)
    block_table = draw_block_table(jax.random.fold_in(key_of[15], 71), 0)
    lengths = draw_lengths(jax.random.fold_in(key_of[15], 71), 0)
    return {"hidden_in": hidden_in, "moe_gain": moe_gain, "router": router, "routes": routes, "gate_weight": gate_weight, "up_weight": up_weight, "down_weight": down_weight, "attn_gain": attn_gain, "kv_weight": kv_weight, "queries": queries, "decode_cache": decode_cache, "prompt_cache": prompt_cache, "handoff": handoff, "block_table": block_table, "lengths": lengths}


epsilon = 1e-06

def rms_scaled(values, gain_row):
    mean_square = lax.optimization_barrier(jnp.mean(values * values, axis=-1, keepdims=True))
    return values * lax.rsqrt(mean_square + epsilon) * gain_row

def slot_numbers(choices_in, expert_total, capacity):
    token_rows, picks_per = choices_in.shape
    flat_ids = choices_in.reshape(token_rows * picks_per)
    expert_ids = jnp.arange(expert_total, dtype=jnp.int32)
    one_hot = (flat_ids[:, None] == expert_ids[None, :]).astype(jnp.int32)
    earlier = jnp.cumsum(one_hot, axis=0) - one_hot
    places = lax.optimization_barrier(jnp.sum(earlier * one_hot, axis=1))
    return (flat_ids * capacity + places).reshape(token_rows, picks_per)

def reference(hidden_in, moe_gain, router, routes, gate_weight, up_weight, down_weight, attn_gain, kv_weight, queries, decode_cache, prompt_cache, handoff, block_table, lengths):
    moe_in = rms_scaled(hidden_in.astype(jnp.float32), moe_gain.astype(jnp.float32)).astype(jnp.bfloat16)
    logits = jnp.dot(moe_in, router, preferred_element_type=jnp.float32)
    gate_probs = jax.nn.softmax(jnp.take_along_axis(logits, routes, axis=1), axis=1)
    group_routes = routes.reshape(GROUPS, ROWS, TOP)
    slot_ids = jax.vmap(lambda one_group: slot_numbers(one_group, EXPERTS, CAP))(group_routes)
    group_inputs = moe_in.reshape(GROUPS, ROWS, D)

    def pack_group(inputs, group_slots):
        buffer = jnp.zeros((EXPERTS * CAP, D), jnp.bfloat16)
        repeated = jnp.repeat(inputs, TOP, axis=0)
        return buffer.at[group_slots.reshape(ROWS * TOP)].set(repeated)
    packed = jax.vmap(pack_group)(group_inputs, slot_ids).reshape(GROUPS, EXPERTS, CAP, D)

    def run_expert(expert):
        inputs = packed[:, expert].reshape(GROUPS * CAP, D)
        gate_full = jnp.concatenate([gate_weight[2 * expert], gate_weight[2 * expert + 1]], axis=1)
        up_full = jnp.concatenate([up_weight[2 * expert], up_weight[2 * expert + 1]], axis=1)
        down_full = jnp.concatenate([down_weight[2 * expert], down_weight[2 * expert + 1]], axis=0)
        gate_act = jnp.dot(inputs, gate_full, preferred_element_type=jnp.float32)
        up_act = jnp.dot(inputs, up_full, preferred_element_type=jnp.float32)
        hidden_act = (jax.nn.silu(gate_act) * up_act).astype(jnp.bfloat16)
        running = jnp.zeros((GROUPS * CAP, D), jnp.float32)
        for run_index in range(MOE_FF // UNITS):
            part_out = jnp.dot(hidden_act[:, run_index * UNITS:(run_index + 1) * UNITS], down_full[run_index * UNITS:(run_index + 1) * UNITS], preferred_element_type=jnp.float32)
            running = running + lax.optimization_barrier(part_out.astype(jnp.bfloat16)).astype(jnp.float32)
        return running.reshape(GROUPS, CAP, D)
    expert_out = lax.map(run_expert, jnp.arange(EXPERTS, dtype=jnp.int32))
    by_group = jnp.moveaxis(expert_out, 0, 1).reshape(GROUPS, EXPERTS * CAP, D)
    picked = jax.vmap(lambda out_table, id_rows: jnp.take(out_table, id_rows, axis=0))(by_group, slot_ids)
    moe_sum = lax.optimization_barrier(jnp.sum(picked * gate_probs.reshape(GROUPS, ROWS, TOP, 1), axis=2)).reshape(TOKENS, D)
    residual_out = hidden_in.astype(jnp.float32) + moe_sum
    attn_in = rms_scaled(residual_out, attn_gain.astype(jnp.float32)).astype(jnp.bfloat16)
    new_kv = jnp.dot(attn_in, kv_weight.reshape(D, 2 * KV_HEADS * HEAD_DIM), preferred_element_type=jnp.float32).astype(jnp.bfloat16).reshape(TOKENS, 2, KV_HEADS * HEAD_DIM)
    per_kv = HEADS // KV_HEADS
    score_scale = HEAD_DIM ** (-0.5)
    cache_span = MAX_BLOCKS * BLOCK

    def attend(group_id):
        pool_index = group_id // PEERS
        group_index = group_id % PEERS
        own_blocks = lax.dynamic_slice_in_dim(decode_cache, group_id * RES_BLOCKS, RES_BLOCKS, 0)
        sources = (1 - pool_index) * PEERS + jnp.arange(PEERS, dtype=jnp.int32)
        chosen = handoff[sources, group_index]
        arrived = jnp.take(prompt_cache, (sources * PEERS + chosen).astype(jnp.int32), axis=0)
        local_pool = jnp.concatenate([own_blocks, arrived], axis=0)
        block_rows = lax.dynamic_slice_in_dim(block_table, group_id * REQ, REQ, 0)
        seen_len = lax.dynamic_slice_in_dim(lengths, group_id * REQ, REQ, 0)
        paged_blocks = jnp.take(local_pool, block_rows.reshape(REQ * MAX_BLOCKS), axis=0).reshape(REQ, MAX_BLOCKS, KV_HEADS, 2, BLOCK, HEAD_DIM)
        paged_blocks = jnp.transpose(paged_blocks, (0, 2, 3, 1, 4, 5)).reshape(REQ, KV_HEADS, 2, cache_span, HEAD_DIM).astype(jnp.float32)
        query_rows = lax.dynamic_slice_in_dim(queries, group_id * ROWS, ROWS, 0).reshape(REQ, DRAFT, KV_HEADS, per_kv, HEAD_DIM)
        query_rows = jnp.transpose(query_rows, (0, 2, 1, 3, 4)).reshape(REQ, KV_HEADS, DRAFT * per_kv, HEAD_DIM).astype(jnp.float32)
        fresh_kv = lax.dynamic_slice_in_dim(new_kv, group_id * ROWS, ROWS, 0).reshape(REQ, DRAFT, 2, KV_HEADS, HEAD_DIM)
        fresh_kv = jnp.transpose(fresh_kv, (0, 3, 2, 1, 4)).astype(jnp.float32)
        cached = jnp.einsum('rhqd,rhkd->rhqk', query_rows, paged_blocks[:, :, 0]) * score_scale
        recent = jnp.einsum('rhqd,rhjd->rhqj', query_rows, fresh_kv[:, :, 0]) * score_scale
        in_length = jnp.arange(cache_span, dtype=jnp.int32)[None, None, None, :] < seen_len[:, None, None, None]
        step_of = jnp.arange(DRAFT * per_kv, dtype=jnp.int32) // per_kv
        causal = (jnp.arange(DRAFT, dtype=jnp.int32)[None, :] <= step_of[:, None])[None, None]
        cached = jnp.where(in_length, cached, -jnp.inf)
        recent = jnp.where(causal, recent, -jnp.inf)
        top_score = jnp.maximum(lax.optimization_barrier(jnp.max(cached, axis=3)), lax.optimization_barrier(jnp.max(recent, axis=3)))[..., None]
        cached_exp = jnp.exp(cached - top_score)
        recent_exp = jnp.exp(recent - top_score)
        denom = lax.optimization_barrier(jnp.sum(cached_exp, axis=3, keepdims=True)) + lax.optimization_barrier(jnp.sum(recent_exp, axis=3, keepdims=True))
        cached_w = lax.optimization_barrier((cached_exp / denom).astype(jnp.bfloat16)).astype(jnp.float32)
        recent_w = lax.optimization_barrier((recent_exp / denom).astype(jnp.bfloat16)).astype(jnp.float32)
        mixed_out = jnp.einsum('rhqk,rhkd->rhqd', cached_w, paged_blocks[:, :, 1]) + jnp.einsum('rhqj,rhjd->rhqd', recent_w, fresh_kv[:, :, 1])
        mixed_out = mixed_out.astype(jnp.bfloat16).reshape(REQ, KV_HEADS, DRAFT, per_kv, HEAD_DIM)
        return jnp.transpose(mixed_out, (0, 2, 1, 3, 4)).reshape(ROWS, HEADS * HEAD_DIM)
    attn_out = lax.map(attend, jnp.arange(GROUPS, dtype=jnp.int32)).reshape(TOKENS, HEADS * HEAD_DIM)
    return (residual_out, new_kv, attn_out)
```

```python
import functools

import jax
import jax.numpy as jnp
from jax import lax
from jax.experimental import pallas as pl
from jax.experimental.pallas import tpu as pltpu
from jax.sharding import PartitionSpec as P

epsilon = 1e-06
LANES = 128


def swapped(x, axis, bit):
    return lax.ppermute(x, axis, [(i, i ^ 1 << bit) for i in range(lax.axis_size(axis))])


def turned(x, step):
    roles, parts = lax.axis_size("role"), lax.axis_size("tp")
    chips = roles * parts // 2
    pairs = []
    for role in range(roles):
        for part in range(parts):
            place = ((part // 2) * roles + role + step) % chips
            pairs.append((role * parts + part, (place % roles) * parts + place // roles * 2 + part % 2))
    return lax.ppermute(x, ("role", "tp"), pairs)


def across(x):
    half = x.shape[0] // 2
    up, down = turned(x[:half], 1), turned(x[half:], -1)
    return turned(up, 1), turned(down, -1)


def inverse_rms(square_sum, width):
    return lax.rsqrt(square_sum / width + epsilon)


def slot_numbers(choices_in, expert_total, capacity):
    token_rows, picks_per = choices_in.shape
    flat_ids = choices_in.reshape(token_rows * picks_per)
    expert_ids = jnp.arange(expert_total, dtype=jnp.int32)
    one_hot = (flat_ids[:, None] == expert_ids[None, :]).astype(jnp.int32)
    earlier = jnp.cumsum(one_hot, axis=0) - one_hot
    places = jnp.sum(earlier * one_hot, axis=1)
    return (flat_ids * capacity + places).reshape(token_rows, picks_per)


def send_slots(slot_ids, capacity):
    expert, place = slot_ids // capacity, slot_ids % capacity
    first = 2 * expert * capacity + place
    return first, first + capacity


def cached_attention(table_ref, length_ref, query_ref, pool_ref, top_ref, total_ref, mixed_ref, *, max_blocks):
    requests, rows, head_dim = query_ref.shape
    block_len = pool_ref.shape[2]
    span = max_blocks * block_len
    scale = head_dim ** (-0.5)
    places = lax.broadcasted_iota(jnp.int32, (rows, span), 1)

    def one(r, carry):
        ids = [table_ref[r * max_blocks + b] for b in range(max_blocks)]
        keys = jnp.concatenate([pool_ref[i, 0] for i in ids], axis=0)
        values = jnp.concatenate([pool_ref[i, 1] for i in ids], axis=0)
        scores = lax.dot_general(
            query_ref[r], keys, (((1,), (1,)), ((), ())), preferred_element_type=jnp.float32
        )
        scores = jnp.where(places < length_ref[r], scores * scale, -jnp.inf)
        top = jnp.max(scores, axis=1, keepdims=True)
        exps = jnp.exp(scores - top)
        total = jnp.sum(exps, axis=1, keepdims=True)
        mixed = jnp.dot(exps.astype(jnp.bfloat16), values, preferred_element_type=jnp.float32)
        top_ref[r] = jnp.broadcast_to(top, (rows, head_dim))
        total_ref[r] = jnp.broadcast_to(total, (rows, head_dim))
        mixed_ref[r] = mixed
        return carry

    lax.fori_loop(0, requests, one, 0, unroll=2)


def attend_cache(block_table, lengths, query_rows, pool):
    requests, rows, head_dim = query_rows.shape
    shape = jax.ShapeDtypeStruct((requests, rows, head_dim), jnp.float32)
    smem = pl.BlockSpec(memory_space=pltpu.SMEM)
    vmem = pl.BlockSpec(memory_space=pltpu.VMEM)
    return pl.pallas_call(
        functools.partial(cached_attention, max_blocks=block_table.shape[1]),
        out_shape=(shape, shape, shape),
        in_specs=[smem, smem, vmem, vmem],
        out_specs=(vmem, vmem, vmem),
        compiler_params=pltpu.CompilerParams(vmem_limit_bytes=40 << 20),
        name="cached_attention",
    )(block_table.reshape(-1), lengths, query_rows, pool)


def local(
    hidden_in,
    moe_gain,
    router,
    routes,
    gate_weight,
    up_weight,
    down_weight,
    attn_gain,
    kv_weight,
    queries,
    decode_cache,
    prompt_cache,
    handoff,
    block_table,
    lengths,
):
    peer_count = lax.axis_size("grp")
    expert_count = peer_count // 2
    tp_count = lax.axis_size("tp")
    tp_rank = lax.axis_index("tp")
    token_rows, model_width = hidden_in.shape
    picks_per = routes.shape[1]
    quarter = model_width // tp_count
    capacity = min(token_rows, 3 * token_rows * picks_per // (2 * expert_count))
    total_slots = 2 * expert_count * capacity
    f32, bf16 = jnp.float32, jnp.bfloat16

    def own(x):
        return lax.dynamic_slice_in_dim(x, tp_rank * quarter, quarter, x.ndim - 1)

    hidden = hidden_in.astype(f32)
    scale_in = inverse_rms(jnp.sum(hidden * hidden, axis=1, keepdims=True), model_width)
    own_hidden = own(hidden_in).astype(f32)
    own_moe = (own_hidden * scale_in * own(moe_gain).astype(f32)).astype(bf16)
    slot_ids = slot_numbers(routes, expert_count, capacity)
    first, second = send_slots(slot_ids, capacity)
    targets = jnp.arange(total_slots, dtype=jnp.int32)
    hits = (first[:, :, None] == targets) | (second[:, :, None] == targets)
    placing = jnp.sum(hits.astype(f32), axis=1).astype(bf16)
    packed = lax.dot_general(
        placing, own_moe, (((0,), (0,)), ((), ())), preferred_element_type=f32
    ).astype(bf16)
    landed = lax.all_to_all(
        packed.reshape(peer_count, capacity, quarter), "grp", split_axis=0, concat_axis=0, tiled=True
    )

    ordered = jnp.take(prompt_cache[:, 0], handoff[0], axis=0)
    crossed = swapped(ordered, "role", 0)
    crossed, landed = lax.optimization_barrier((crossed, landed))
    arrived = lax.all_to_all(crossed, "grp", split_axis=0, concat_axis=0, tiled=True)

    moe_in = (hidden * scale_in * moe_gain.astype(f32)).astype(bf16)
    logits = jnp.dot(moe_in, router, preferred_element_type=f32)
    gate_probs = jax.nn.softmax(jnp.take_along_axis(logits, routes, axis=1), axis=1)
    combine = jnp.sum(hits.astype(f32) * gate_probs[:, :, None], axis=1)
    combine_high = combine.astype(bf16)
    combine_low = (combine - combine_high.astype(f32)).astype(bf16)

    landed = landed.reshape(total_slots, quarter)
    gate_own, up_own, down_own = gate_weight[0], up_weight[0], down_weight[0]

    def rows_of(weight, part):
        return lax.dynamic_slice_in_dim(weight, part * quarter, quarter, 0)

    def first_half(inputs, part):
        return (
            jnp.dot(inputs, rows_of(gate_own, part), preferred_element_type=f32),
            jnp.dot(inputs, rows_of(up_own, part), preferred_element_type=f32),
        )

    beside = swapped(landed, "tp", 0)
    opposite = jnp.concatenate(across(landed), axis=0)
    diagonal = swapped(opposite, "tp", 0)
    acts = [
        first_half(landed, tp_rank),
        first_half(beside, tp_rank ^ 1),
        first_half(opposite, tp_rank ^ 2),
        first_half(diagonal, tp_rank ^ 3),
    ]
    gate_act = (acts[0][0] + acts[1][0]) + (acts[2][0] + acts[3][0])
    up_act = (acts[0][1] + acts[1][1]) + (acts[2][1] + acts[3][1])
    hidden_act = (jax.nn.silu(gate_act) * up_act).astype(bf16)

    def second_half(part):
        columns = lax.dynamic_slice_in_dim(down_own, part * quarter, quarter, 1)
        return jnp.dot(hidden_act, columns, preferred_element_type=f32).astype(bf16)

    far = second_half(tp_rank ^ 2).astype(f32) + swapped(second_half(tp_rank ^ 3), "tp", 0).astype(f32)
    far = jnp.concatenate(across(far.astype(bf16)), axis=0)
    near = second_half(tp_rank).astype(f32) + swapped(second_half(tp_rank ^ 1), "tp", 0).astype(f32)
    summed = (near + far.astype(f32)).astype(bf16)
    returned = lax.all_to_all(
        summed.reshape(peer_count, capacity, quarter), "grp", split_axis=0, concat_axis=0, tiled=True
    ).reshape(total_slots, quarter)
    moe_sum = jnp.dot(combine_high, returned, preferred_element_type=f32) + jnp.dot(
        combine_low, returned, preferred_element_type=f32
    )
    residual_out = own_hidden + moe_sum

    requests, max_blocks = block_table.shape
    head_dim = kv_weight.shape[2]
    draft_count = token_rows // requests
    per_kv = queries.shape[1] // head_dim
    query_rows = queries.reshape(requests, draft_count * per_kv, head_dim)
    pool = jnp.concatenate([decode_cache[:, 0], arrived], axis=0)
    top, total, mixed = attend_cache(block_table, lengths, query_rows, pool)

    own_scaled = (residual_out * own(attn_gain).astype(f32)).astype(bf16)
    own_squares = jnp.sum(residual_out * residual_out, axis=1, keepdims=True)
    squares_high = own_squares.astype(bf16)
    squares_mid = (own_squares - squares_high.astype(f32)).astype(bf16)
    lane = lax.broadcasted_iota(jnp.int32, (token_rows, LANES), 1)
    extra = jnp.where(lane == 0, squares_high, jnp.where(lane == 1, squares_mid, jnp.zeros((), bf16)))
    gathered = lax.all_gather(jnp.concatenate([own_scaled, extra], axis=1), "tp", axis=0)
    squares = jnp.sum(gathered[:, :, quarter : quarter + 2].astype(f32), axis=(0, 2))[:, None]
    weight = kv_weight.reshape(tp_count, quarter, 2 * head_dim)
    fresh = sum(
        jnp.dot(gathered[i, :, :quarter], weight[i], preferred_element_type=f32) for i in range(tp_count)
    )
    fresh_kv = (fresh * inverse_rms(squares, model_width)).astype(bf16)
    new_kv = fresh_kv.reshape(token_rows, 2, head_dim)

    flat_rows = requests * draft_count * per_kv
    flat_queries = query_rows.reshape(flat_rows, head_dim)
    recent = lax.dot_general(
        flat_queries, fresh_kv[:, :head_dim], (((1,), (1,)), ((), ())), preferred_element_type=f32
    ) * (head_dim ** (-0.5))
    row = lax.broadcasted_iota(jnp.int32, (flat_rows, token_rows), 0) // per_kv
    col = lax.broadcasted_iota(jnp.int32, (flat_rows, token_rows), 1)
    seen = (row // draft_count == col // draft_count) & (col <= row)
    recent = jnp.where(seen, recent, -jnp.inf)
    top = top.reshape(flat_rows, head_dim)[:, :1]
    total = total.reshape(flat_rows, head_dim)[:, :1]
    mixed = mixed.reshape(flat_rows, head_dim)
    new_top = jnp.maximum(top, jnp.max(recent, axis=1, keepdims=True))
    recent_exp = jnp.exp(recent - new_top)
    shrink = jnp.exp(top - new_top)
    denom = shrink * total + jnp.sum(recent_exp, axis=1, keepdims=True)
    out = mixed * (shrink / denom) + jnp.dot(
        (recent_exp / denom).astype(bf16), fresh_kv[:, head_dim:], preferred_element_type=f32
    )
    attn_out = out.astype(bf16).reshape(token_rows, per_kv * head_dim)
    return (residual_out, new_kv, attn_out)


def solution(mesh):
    in_specs = (
        P(("role", "grp"), None),
        P(),
        P(),
        P(("role", "grp"), None),
        P("grp", None, "tp"),
        P("grp", None, "tp"),
        P("grp", "tp", None),
        P(),
        P(None, None, "tp"),
        P(("role", "grp"), "tp"),
        P(("role", "grp"), "tp", None, None, None),
        P(("role", "grp"), "tp", None, None, None),
        P(("role", "grp"), None),
        P(("role", "grp"), None),
        P(("role", "grp")),
    )
    out_specs = (P(("role", "grp"), "tp"), P(("role", "grp"), None, "tp"), P(("role", "grp"), "tp"))
    return jax.shard_map(local, mesh=mesh, in_specs=in_specs, out_specs=out_specs, check_vma=False)
```

```python
import functools

import jax
import jax.numpy as jnp
from jax import lax
from jax.experimental import pallas as pl
from jax.experimental.pallas import tpu as pltpu
from jax.sharding import PartitionSpec as P

epsilon = 1e-06
LANES = 128


def swapped(x, axis, bit):
    return lax.ppermute(x, axis, [(i, i ^ 1 << bit) for i in range(lax.axis_size(axis))])


def turned(x, step):
    roles, parts = lax.axis_size("role"), lax.axis_size("tp")
    chips = roles * parts // 2
    pairs = []
    for role in range(roles):
        for part in range(parts):
            place = ((part // 2) * roles + role + step) % chips
            pairs.append((role * parts + part, (place % roles) * parts + place // roles * 2 + part % 2))
    return lax.ppermute(x, ("role", "tp"), pairs)


def across(x):
    half = x.shape[0] // 2
    up, down = turned(x[:half], 1), turned(x[half:], -1)
    return turned(up, 1), turned(down, -1)


def inverse_rms(square_sum, width):
    return lax.rsqrt(square_sum / width + epsilon)


def prepare(part_ref, routes_ref, hidden_ref, gain_ref, ordered_ref, packed_ref, slots_ref, *, capacity):
    token_rows, model_width = hidden_ref.shape
    peers, _, eighth = packed_ref.shape
    experts = peers // 2
    quarter = 2 * eighth
    f32, bf16 = jnp.float32, jnp.bfloat16
    hidden = hidden_ref[...].astype(f32)
    squares = jnp.sum(hidden * hidden, axis=1, keepdims=True)
    columns = pl.ds(pl.multiple_of(part_ref[0] * quarter, quarter), quarter)
    own = hidden_ref[:, columns].astype(f32) * inverse_rms(squares, model_width) * gain_ref[:, columns].astype(f32)
    one_routes, two_routes = routes_ref[0:1, :], routes_ref[1:2, :]
    expert = lax.broadcasted_iota(jnp.int32, (max(experts, 8), token_rows), 0)
    one_hot, two_hot = (expert == one_routes).astype(f32), (expert == two_routes).astype(f32)
    before = lax.broadcasted_iota(jnp.int32, (token_rows, token_rows), 0) < lax.broadcasted_iota(
        jnp.int32, (token_rows, token_rows), 1
    )
    taken = jnp.dot((one_hot + two_hot).astype(bf16), before.astype(f32).astype(bf16), preferred_element_type=f32)
    one_slot = one_routes * capacity + jnp.sum(taken * one_hot, axis=0, keepdims=True).astype(jnp.int32)
    two_slot = two_routes * capacity + jnp.sum(taken * two_hot, axis=0, keepdims=True).astype(jnp.int32)
    slots_ref[0:1, :] = one_slot
    slots_ref[1:2, :] = two_slot
    target = lax.broadcasted_iota(jnp.int32, (experts * capacity, token_rows), 0)
    placing = ((target == one_slot) | (target == two_slot)).astype(f32).astype(bf16)
    packed = jnp.dot(placing, own.astype(bf16), preferred_element_type=f32)
    for e in range(experts):
        for half in range(2):
            block = packed[e * capacity : (e + 1) * capacity, half * eighth : (half + 1) * eighth]
            packed_ref[2 * e + half] = block.astype(bf16)


def expert_units(blocks_ref, *refs):
    f32, bf16 = jnp.float32, jnp.bfloat16
    inputs, (gate_ref, up_ref, down_ref), outputs = refs[:12], refs[12:15], refs[15:]
    rows, eighth = outputs[0].shape
    half = rows // 2

    def window(i):
        return pl.ds(pl.multiple_of(blocks_ref[i] * eighth, eighth), eighth)

    for part in range(2):
        span = slice(part * half, (part + 1) * half)
        gate = up = None
        for core in range(2):
            own, side, y_low, y_high, d_low, d_high = inputs[6 * core : 6 * core + 6]
            pieces = (own[span], side[span], (y_low, y_high)[part][...], (d_low, d_high)[part][...])
            for i, piece in enumerate(pieces):
                more_gate = jnp.dot(piece, gate_ref[window(4 * core + i), :], preferred_element_type=f32)
                more_up = jnp.dot(piece, up_ref[window(4 * core + i), :], preferred_element_type=f32)
                gate = more_gate if gate is None else gate + more_gate
                up = more_up if up is None else up + more_up
        act = (gate / (1.0 + jnp.exp(-gate)) * up).astype(bf16)
        for i in range(8):
            outputs[i][span] = jnp.dot(act, down_ref[:, window(i)], preferred_element_type=f32).astype(bf16)


def join(near_ref, x_ref, y_low_ref, y_high_ref, *refs):
    out_ref = refs[-1]
    half = y_low_ref.shape[0]
    for part, y_ref in enumerate((y_low_ref, y_high_ref)):
        span = slice(part * half, (part + 1) * half)
        total = near_ref[span].astype(jnp.float32) + x_ref[span].astype(jnp.float32) + y_ref[...].astype(jnp.float32)
        out_ref[span] = total.astype(out_ref.dtype)


def finish(part_ref, combine_ref, returned_ref, hidden_ref, gain_ref, residual_ref, scaled_ref):
    f32, bf16 = jnp.float32, jnp.bfloat16
    token_rows = hidden_ref.shape[0]
    eighth = returned_ref.shape[1]
    quarter = 2 * eighth
    squares = jnp.zeros((token_rows, 1), f32)
    for half in range(2):
        start = pl.multiple_of(part_ref[0] * quarter + half * eighth, eighth)
        terms = jnp.dot(combine_ref[half], returned_ref[...], preferred_element_type=f32)
        moe = terms[:token_rows] + terms[token_rows:]
        value = hidden_ref[:, pl.ds(start, eighth)].astype(f32) + moe
        residual_ref[:, half * eighth : (half + 1) * eighth] = value
        scaled_ref[:, half * eighth : (half + 1) * eighth] = (value * gain_ref[:, pl.ds(start, eighth)].astype(f32)).astype(bf16)
        squares = squares + jnp.sum(value * value, axis=1, keepdims=True)
    high = squares.astype(bf16).astype(f32)
    lane = lax.broadcasted_iota(jnp.int32, (token_rows, LANES), 1)
    extra = jnp.where(lane == 0, high, jnp.where(lane == 1, squares - high, 0.0))
    scaled_ref[:, quarter:] = extra.astype(bf16)


def last_step(part_ref, own_ref, core_ref, y_ref, diagonal_ref, weight_ref, query_ref, top_ref, total_ref, mixed_ref, kv_ref, out_ref, *, draft):
    f32, bf16 = jnp.float32, jnp.bfloat16
    token_rows = query_ref.shape[0]
    head_dim = kv_ref.shape[1] // 2
    quarter = own_ref.shape[1] - LANES
    parts = (own_ref, core_ref, y_ref, diagonal_ref)
    squares = jnp.zeros((token_rows, LANES), f32)
    fresh = jnp.zeros((token_rows, 2 * head_dim), f32)
    for i, ref in enumerate(parts):
        rows = pl.ds(pl.multiple_of((part_ref[0] ^ i) * quarter, quarter), quarter)
        fresh = fresh + jnp.dot(ref[:, :quarter], weight_ref[rows, :], preferred_element_type=f32)
        squares = squares + ref[:, quarter:].astype(f32)
    square_sum = jnp.sum(squares, axis=1, keepdims=True)
    fresh = (fresh * inverse_rms(square_sum, len(parts) * quarter)).astype(bf16)
    kv_ref[...] = fresh
    keys, values = fresh[:, :head_dim], fresh[:, head_dim:]
    row = lax.broadcasted_iota(jnp.int32, (token_rows, token_rows), 0)
    col = lax.broadcasted_iota(jnp.int32, (token_rows, token_rows), 1)
    seen = (row // draft == col // draft) & (col <= row)
    for h in range(query_ref.shape[1] // head_dim):
        lanes = slice(h * head_dim, (h + 1) * head_dim)
        scores = lax.dot_general(
            query_ref[:, lanes], keys, (((1,), (1,)), ((), ())), preferred_element_type=f32
        )
        scores = jnp.where(seen, scores * head_dim ** (-0.5), -jnp.inf)
        top = top_ref[:, lanes][:, :1]
        new_top = jnp.maximum(top, jnp.max(scores, axis=1, keepdims=True))
        exps = jnp.exp(scores - new_top)
        shrink = jnp.exp(top - new_top)
        denom = shrink * total_ref[:, lanes][:, :1] + jnp.sum(exps, axis=1, keepdims=True)
        mixed = mixed_ref[:, lanes] * (shrink / denom)
        mixed = mixed + jnp.dot((exps / denom).astype(bf16), values, preferred_element_type=f32)
        out_ref[:, lanes] = mixed.astype(bf16)


def call(kernel, out_shape, args, smem=0, name=None, away=0, flops=0):
    spaces = [pltpu.SMEM] * smem + [pltpu.VMEM] * (len(args) - smem - away) + [pl.ANY] * away
    out_specs = jax.tree.map(lambda _: pl.BlockSpec(memory_space=pltpu.VMEM), out_shape)
    moved = sum(x.size * x.dtype.itemsize for x in list(args) + jax.tree.leaves(out_shape))
    return pl.pallas_call(
        kernel,
        out_shape=out_shape,
        in_specs=[pl.BlockSpec(memory_space=space) for space in spaces],
        out_specs=out_specs,
        compiler_params=pltpu.CompilerParams(vmem_limit_bytes=48 << 20),
        cost_estimate=pl.CostEstimate(flops=flops, transcendentals=0, bytes_accessed=moved),
        name=name,
    )(*args)


def cached_attention(table_ref, length_ref, query_ref, pool_ref, top_ref, total_ref, mixed_ref, *, max_blocks):
    requests, rows, head_dim = query_ref.shape
    block_len = pool_ref.shape[2]
    span = max_blocks * block_len
    scale = head_dim ** (-0.5)
    places = lax.broadcasted_iota(jnp.int32, (rows, span), 1)

    def one(r, carry):
        ids = [table_ref[r * max_blocks + b] for b in range(max_blocks)]
        keys = jnp.concatenate([pool_ref[i, 0] for i in ids], axis=0)
        values = jnp.concatenate([pool_ref[i, 1] for i in ids], axis=0)
        scores = lax.dot_general(
            query_ref[r], keys, (((1,), (1,)), ((), ())), preferred_element_type=jnp.float32
        )
        scores = jnp.where(places < length_ref[r], scores * scale, -jnp.inf)
        top = jnp.max(scores, axis=1, keepdims=True)
        exps = jnp.exp(scores - top)
        total = jnp.sum(exps, axis=1, keepdims=True)
        mixed = jnp.dot(exps.astype(jnp.bfloat16), values, preferred_element_type=jnp.float32)
        top_ref[r] = jnp.broadcast_to(top, (rows, head_dim))
        total_ref[r] = jnp.broadcast_to(total, (rows, head_dim))
        mixed_ref[r] = mixed
        return carry

    lax.fori_loop(0, requests, one, 0, unroll=2)


def local(
    hidden_in,
    moe_gain,
    router,
    routes,
    gate_weight,
    up_weight,
    down_weight,
    attn_gain,
    kv_weight,
    queries,
    decode_cache,
    prompt_cache,
    handoff,
    block_table,
    lengths,
):
    peer_count = lax.axis_size("grp")
    expert_count = peer_count // 2
    tp_count = lax.axis_size("tp")
    tp_rank = lax.axis_index("tp")
    token_rows, model_width = hidden_in.shape
    picks_per = routes.shape[1]
    quarter = model_width // tp_count
    capacity = min(token_rows, 3 * token_rows * picks_per // (2 * expert_count))
    total_slots = 2 * expert_count * capacity
    eighth = quarter // 2
    f32, bf16 = jnp.float32, jnp.bfloat16
    shape = jax.ShapeDtypeStruct
    side = lax.axis_index("grp") & 1
    part = tp_rank.astype(jnp.int32).reshape(1)

    ordered = jnp.take(prompt_cache[:, 0], handoff[0], axis=0)
    crossed = swapped(ordered, "role", 0)

    packed, slots = call(
        functools.partial(prepare, capacity=capacity),
        (shape((peer_count, capacity, eighth), bf16), shape((picks_per, token_rows), jnp.int32)),
        (part, routes.T, hidden_in, moe_gain.reshape(1, model_width), ordered),
        smem=1,
        away=1,
        name="prepare",
    )
    landed = lax.all_to_all(packed, "grp", split_axis=0, concat_axis=0, tiled=True)
    landed = landed.reshape(total_slots, eighth)

    arrived = lax.all_to_all(crossed, "grp", split_axis=0, concat_axis=0, tiled=True)

    hidden = hidden_in.astype(f32)
    scale_in = inverse_rms(jnp.sum(hidden * hidden, axis=1, keepdims=True), model_width)
    moe_in = (hidden * scale_in * moe_gain.astype(f32)).astype(bf16)
    logits = jnp.dot(moe_in, router, preferred_element_type=f32)
    gate_probs = jax.nn.softmax(jnp.take_along_axis(logits, routes, axis=1), axis=1)
    targets = jnp.arange(total_slots, dtype=jnp.int32)
    target_slot = targets // (2 * capacity) * capacity + targets % capacity
    hits = (slots.T[:, :, None] == target_slot).astype(f32)
    combine = jnp.sum(hits * gate_probs[:, :, None], axis=1)
    combine_high = combine.astype(bf16)
    combine_low = (combine - combine_high.astype(f32)).astype(bf16)
    both_terms = jnp.concatenate([combine_high, combine_low], axis=0)
    target_half = targets // capacity % 2
    halves = jnp.stack([jnp.where(target_half == i, both_terms, jnp.zeros((), bf16)) for i in range(2)])

    from_x = swapped(landed, "grp", 0)
    y_low, y_high = across(landed)
    d_low, d_high = swapped(y_low, "grp", 0), swapped(y_high, "grp", 0)
    mine = (landed, from_x, y_low, y_high, d_low, d_high)
    theirs = tuple(swapped(x, "tp", 0) for x in mine)
    blocks = jnp.stack(
        [
            (tp_rank ^ (core + 2 * y)) * 2 + (side ^ x)
            for core in range(2)
            for y, x in ((0, 0), (0, 1), (1, 0), (1, 1))
        ]
    ).astype(jnp.int32)
    sums = call(
        expert_units,
        (shape((total_slots, eighth), bf16),) * 8,
        (blocks, *mine, *theirs, gate_weight[0], up_weight[0], down_weight[0]),
        smem=1,
        name="expert_units",
        flops=6 * total_slots * model_width * gate_weight.shape[2],
    )

    def both_cores(i):
        return sums[i].astype(f32) + swapped(sums[4 + i], "tp", 0).astype(f32)

    far = swapped(both_cores(3).astype(bf16), "grp", 0)
    far = (both_cores(2) + far.astype(f32)).astype(bf16)
    sum_x = swapped(both_cores(1).astype(bf16), "grp", 0)
    sum_low, sum_high = across(far)
    near = both_cores(0).astype(bf16)

    requests, max_blocks = block_table.shape
    head_dim = kv_weight.shape[2]
    draft_count = token_rows // requests
    per_kv = queries.shape[1] // head_dim
    query_rows = queries.reshape(requests, draft_count * per_kv, head_dim)
    pool = jnp.concatenate([decode_cache[:, 0], arrived], axis=0)
    stats = call(
        functools.partial(cached_attention, max_blocks=max_blocks),
        (shape((requests, draft_count * per_kv, head_dim), f32),) * 3,
        (block_table.reshape(-1), lengths, query_rows, pool),
        smem=2,
        name="cached_attention",
        flops=4 * requests * draft_count * per_kv * head_dim * max_blocks * decode_cache.shape[3],
    )
    stats = tuple(x.reshape(token_rows, per_kv * head_dim) for x in stats)
    summed = call(
        join,
        shape((total_slots, eighth), bf16),
        (near, sum_x, sum_low, sum_high, *stats),
        away=3,
        name="join",
    )
    returned = lax.all_to_all(
        summed.reshape(peer_count, capacity, eighth), "grp", split_axis=0, concat_axis=0, tiled=True
    ).reshape(total_slots, eighth)
    residual_out, scaled = call(
        finish,
        (shape((token_rows, quarter), f32), shape((token_rows, quarter + LANES), bf16)),
        (part, halves, returned, hidden_in, attn_gain.reshape(1, model_width)),
        smem=1,
        name="finish",
    )

    scaled_core = swapped(scaled, "tp", 0)
    scaled_y = swapped(scaled, "tp", 1)
    scaled_diagonal = swapped(scaled_y, "tp", 0)
    fresh_kv, attn_out = call(
        functools.partial(last_step, draft=draft_count),
        (shape((token_rows, 2 * head_dim), bf16), shape((token_rows, per_kv * head_dim), bf16)),
        (part, scaled, scaled_core, scaled_y, scaled_diagonal, kv_weight.reshape(model_width, 2 * head_dim), queries, *stats),
        smem=1,
        name="last_step",
    )
    return (residual_out, fresh_kv.reshape(token_rows, 2, head_dim), attn_out)


def solution(mesh):
    in_specs = (
        P(("role", "grp"), None),
        P(),
        P(),
        P(("role", "grp"), None),
        P("grp", None, "tp"),
        P("grp", None, "tp"),
        P("grp", "tp", None),
        P(),
        P(None, None, "tp"),
        P(("role", "grp"), "tp"),
        P(("role", "grp"), "tp", None, None, None),
        P(("role", "grp"), "tp", None, None, None),
        P(("role", "grp"), None),
        P(("role", "grp"), None),
        P(("role", "grp")),
    )
    out_specs = (P(("role", "grp"), "tp"), P(("role", "grp"), None, "tp"), P(("role", "grp"), "tp"))
    return jax.shard_map(local, mesh=mesh, in_specs=in_specs, out_specs=out_specs, check_vma=False)
```

```python
import functools

import jax
import jax.numpy as jnp
from jax import lax
from jax.experimental import pallas as pl
from jax.experimental.pallas import tpu as pltpu
from jax.sharding import PartitionSpec as P

epsilon = 1e-06
LANES = 128


def swapped(x, axis, bit):
    return lax.ppermute(x, axis, [(i, i ^ 1 << bit) for i in range(lax.axis_size(axis))])


def inverse_rms(square_sum, width):
    return lax.rsqrt(square_sum / width + epsilon)


def prepare(part_ref, routes_ref, hidden_ref, gain_ref, packed_ref, slots_ref, *, capacity):
    token_rows, model_width = hidden_ref.shape
    peers, _, eighth = packed_ref.shape
    experts = peers // 2
    quarter = 2 * eighth
    f32, bf16 = jnp.float32, jnp.bfloat16
    hidden = hidden_ref[...].astype(f32)
    squares = jnp.sum(hidden * hidden, axis=1, keepdims=True)
    columns = pl.ds(pl.multiple_of(part_ref[0] * quarter, quarter), quarter)
    own = hidden_ref[:, columns].astype(f32) * inverse_rms(squares, model_width) * gain_ref[:, columns].astype(f32)
    one_routes, two_routes = routes_ref[0:1, :], routes_ref[1:2, :]
    expert = lax.broadcasted_iota(jnp.int32, (max(experts, 8), token_rows), 0)
    one_hot, two_hot = (expert == one_routes).astype(f32), (expert == two_routes).astype(f32)
    before = lax.broadcasted_iota(jnp.int32, (token_rows, token_rows), 0) < lax.broadcasted_iota(
        jnp.int32, (token_rows, token_rows), 1
    )
    taken = jnp.dot((one_hot + two_hot).astype(bf16), before.astype(f32).astype(bf16), preferred_element_type=f32)
    one_slot = one_routes * capacity + jnp.sum(taken * one_hot, axis=0, keepdims=True).astype(jnp.int32)
    two_slot = two_routes * capacity + jnp.sum(taken * two_hot, axis=0, keepdims=True).astype(jnp.int32)
    slots_ref[0:1, :] = one_slot
    slots_ref[1:2, :] = two_slot
    target = lax.broadcasted_iota(jnp.int32, (experts * capacity, token_rows), 0)
    placing = ((target == one_slot) | (target == two_slot)).astype(f32).astype(bf16)
    packed = jnp.dot(placing, own.astype(bf16), preferred_element_type=f32)
    for e in range(experts):
        for half in range(2):
            block = packed[e * capacity : (e + 1) * capacity, half * eighth : (half + 1) * eighth]
            packed_ref[2 * e + half] = block.astype(bf16)


def wide(a, b):
    return lax.dot_general(a, b, (((1,), (1,)), ((), ())), preferred_element_type=jnp.float32)


def window(blocks_ref, i, size):
    return pl.ds(pl.multiple_of(blocks_ref[i] * size, size), size)


def early_units(blocks_ref, *refs):
    pieces, (gate_ref, up_ref, gate_out, up_out) = refs[:6], refs[6:]
    eighth = pieces[0].shape[1]
    for weight, out in ((gate_ref, gate_out), (up_ref, up_out)):
        total = None
        for i, piece in enumerate(pieces):
            more = wide(piece[...], weight[:, window(blocks_ref, 4 * (i // 3) + i % 3, eighth)])
            total = more if total is None else total + more
        out[...] = total


def late_units(blocks_ref, mine_ref, theirs_ref, gate_sum, up_sum, gate_ref, up_ref, down_ref, *refs):
    outputs = refs[-8:]
    eighth = mine_ref.shape[1]
    gate, up = gate_sum[...], up_sum[...]
    for i, piece in ((3, mine_ref), (7, theirs_ref)):
        gate = gate + wide(piece[...], gate_ref[:, window(blocks_ref, i, eighth)])
        up = up + wide(piece[...], up_ref[:, window(blocks_ref, i, eighth)])
    act = (gate / (1.0 + jnp.exp(-gate)) * up).astype(jnp.bfloat16)
    for i in (3, 7, 2, 6, 1, 5, 0, 4):
        columns = down_ref[:, window(blocks_ref, i, eighth)]
        outputs[i][...] = jnp.dot(act, columns, preferred_element_type=jnp.float32).astype(jnp.bfloat16)


def join(mine_ref, theirs_ref, x_ref, y_ref, *refs):
    total = mine_ref[...].astype(jnp.float32) + theirs_ref[...].astype(jnp.float32)
    total = total + x_ref[...].astype(jnp.float32) + y_ref[...].astype(jnp.float32)
    refs[-1][...] = total.astype(jnp.bfloat16)


def held_until(x, other):
    def kernel(x_ref, other_ref, out_ref):
        pass

    any_space = pl.BlockSpec(memory_space=pl.ANY)
    return pl.pallas_call(
        kernel,
        out_shape=jax.ShapeDtypeStruct(x.shape, x.dtype),
        in_specs=[any_space, any_space],
        out_specs=any_space,
        input_output_aliases={0: 0},
        name="held_until",
    )(x, other)


def finish(part_ref, combine_ref, returned_ref, hidden_ref, gain_ref, *refs):
    f32, bf16 = jnp.float32, jnp.bfloat16
    residual_ref, scaled_ref = refs[-2:]
    token_rows = hidden_ref.shape[0]
    eighth = returned_ref.shape[1]
    quarter = 2 * eighth
    squares = jnp.zeros((token_rows, 1), f32)
    for half in range(2):
        start = pl.multiple_of(part_ref[0] * quarter + half * eighth, eighth)
        terms = jnp.dot(combine_ref[half], returned_ref[...], preferred_element_type=f32)
        moe = terms[:token_rows] + terms[token_rows:]
        value = hidden_ref[:, pl.ds(start, eighth)].astype(f32) + moe
        residual_ref[:, half * eighth : (half + 1) * eighth] = value
        scaled_ref[:, half * eighth : (half + 1) * eighth] = (value * gain_ref[:, pl.ds(start, eighth)].astype(f32)).astype(bf16)
        squares = squares + jnp.sum(value * value, axis=1, keepdims=True)
    high = squares.astype(bf16).astype(f32)
    lane = lax.broadcasted_iota(jnp.int32, (token_rows, LANES), 1)
    extra = jnp.where(lane == 0, high, jnp.where(lane == 1, squares - high, 0.0))
    scaled_ref[:, quarter:] = extra.astype(bf16)


def last_step(part_ref, own_ref, core_ref, y_ref, diagonal_ref, weight_ref, query_ref, top_ref, total_ref, mixed_ref, kv_ref, out_ref, *, draft):
    f32, bf16 = jnp.float32, jnp.bfloat16
    token_rows = query_ref.shape[0]
    head_dim = kv_ref.shape[1] // 2
    quarter = own_ref.shape[1] - LANES
    parts = (own_ref, core_ref, y_ref, diagonal_ref)
    squares = jnp.zeros((token_rows, LANES), f32)
    fresh = jnp.zeros((token_rows, 2 * head_dim), f32)
    for i, ref in enumerate(parts):
        rows = pl.ds(pl.multiple_of((part_ref[0] ^ i) * quarter, quarter), quarter)
        fresh = fresh + jnp.dot(ref[:, :quarter], weight_ref[rows, :], preferred_element_type=f32)
        squares = squares + ref[:, quarter:].astype(f32)
    square_sum = jnp.sum(squares, axis=1, keepdims=True)
    fresh = (fresh * inverse_rms(square_sum, len(parts) * quarter)).astype(bf16)
    kv_ref[...] = fresh
    keys = fresh[:, :head_dim]
    values = jnp.concatenate([fresh[:, head_dim:], jnp.ones((token_rows, head_dim), bf16)], axis=1)
    row = lax.broadcasted_iota(jnp.int32, (token_rows, token_rows), 0)
    col = lax.broadcasted_iota(jnp.int32, (token_rows, token_rows), 1)
    seen = (row // draft == col // draft) & (col <= row)
    for h in range(query_ref.shape[1] // head_dim):
        lanes = slice(h * head_dim, (h + 1) * head_dim)
        scores = jnp.where(seen, wide(query_ref[:, lanes], keys) * head_dim ** (-0.5), -jnp.inf)
        top = top_ref[:, lanes]
        new_top = jnp.maximum(top, jnp.max(scores, axis=1, keepdims=True))
        shrink = jnp.exp(top - new_top)
        recent = jnp.dot(jnp.exp(scores - new_top).astype(bf16), values, preferred_element_type=f32)
        denom = shrink * total_ref[:, lanes] + recent[:, head_dim:]
        out_ref[:, lanes] = ((mixed_ref[:, lanes] * shrink + recent[:, :head_dim]) / denom).astype(bf16)


def call(kernel, out_shape, args, smem=0, name=None, away=0, flops=0):
    spaces = [pltpu.SMEM] * smem + [pltpu.VMEM] * (len(args) - smem - away) + [pl.ANY] * away
    out_specs = jax.tree.map(lambda _: pl.BlockSpec(memory_space=pltpu.VMEM), out_shape)
    moved = sum(x.size * x.dtype.itemsize for x in list(args) + jax.tree.leaves(out_shape))
    return pl.pallas_call(
        kernel,
        out_shape=out_shape,
        in_specs=[pl.BlockSpec(memory_space=space) for space in spaces],
        out_specs=out_specs,
        compiler_params=pltpu.CompilerParams(vmem_limit_bytes=48 << 20),
        cost_estimate=pl.CostEstimate(flops=flops, transcendentals=0, bytes_accessed=moved),
        name=name,
    )(*args)


def cached_attention(table_ref, length_ref, query_ref, pool_ref, top_ref, total_ref, mixed_ref, *, max_blocks):
    requests, rows, head_dim = query_ref.shape
    block_len = pool_ref.shape[2]
    span = max_blocks * block_len
    scale = head_dim ** (-0.5)
    places = lax.broadcasted_iota(jnp.int32, (rows, span), 1)
    ones = jnp.ones((span, head_dim), jnp.bfloat16)

    def one(r, carry):
        ids = [table_ref[r * max_blocks + b] for b in range(max_blocks)]
        keys = jnp.concatenate([pool_ref[i, 0] for i in ids], axis=0)
        values = jnp.concatenate([pool_ref[i, 1] for i in ids], axis=0)
        values = jnp.concatenate([values, ones], axis=1)
        scores = lax.dot_general(
            query_ref[r], keys, (((1,), (1,)), ((), ())), preferred_element_type=jnp.float32
        )
        scores = jnp.where(places < length_ref[r], scores * scale, -jnp.inf)
        top = jnp.max(scores, axis=1, keepdims=True)
        exps = jnp.exp(scores - top)
        mixed = jnp.dot(exps.astype(jnp.bfloat16), values, preferred_element_type=jnp.float32)
        top_ref[r] = jnp.broadcast_to(top, (rows, head_dim))
        total_ref[r] = mixed[:, head_dim:]
        mixed_ref[r] = mixed[:, :head_dim]
        return carry

    lax.fori_loop(0, requests, one, 0, unroll=2)


def local(
    hidden_in,
    moe_gain,
    router,
    routes,
    gate_weight,
    up_weight,
    down_weight,
    attn_gain,
    kv_weight,
    queries,
    decode_cache,
    prompt_cache,
    handoff,
    block_table,
    lengths,
):
    peer_count = lax.axis_size("grp")
    expert_count = peer_count // 2
    tp_count = lax.axis_size("tp")
    tp_rank = lax.axis_index("tp")
    token_rows, model_width = hidden_in.shape
    picks_per = routes.shape[1]
    quarter = model_width // tp_count
    capacity = min(token_rows, 3 * token_rows * picks_per // (2 * expert_count))
    total_slots = 2 * expert_count * capacity
    eighth = quarter // 2
    f32, bf16 = jnp.float32, jnp.bfloat16
    shape = jax.ShapeDtypeStruct
    side = lax.axis_index("grp") & 1
    part = tp_rank.astype(jnp.int32).reshape(1)

    packed, slots = call(
        functools.partial(prepare, capacity=capacity),
        (shape((peer_count, capacity, eighth), bf16), shape((picks_per, token_rows), jnp.int32)),
        (part, routes.T, hidden_in, moe_gain.reshape(1, model_width)),
        smem=1,
        name="prepare",
    )
    landed = lax.all_to_all(packed, "grp", split_axis=0, concat_axis=0, tiled=True)
    landed = landed.reshape(total_slots, eighth)

    ordered = prompt_cache[:, 0].at[handoff[0]].get(mode="promise_in_bounds")
    middle = peer_count // 2
    crossed = swapped(ordered[:middle], "role", 0)
    landed = held_until(landed, crossed)

    hidden = hidden_in.astype(f32)
    scale_in = inverse_rms(jnp.sum(hidden * hidden, axis=1, keepdims=True), model_width)
    moe_in = (hidden * scale_in * moe_gain.astype(f32)).astype(bf16)
    logits = jnp.dot(moe_in, router, preferred_element_type=f32)
    gate_probs = jax.nn.softmax(jnp.take_along_axis(logits, routes, axis=1), axis=1)
    targets = jnp.arange(total_slots, dtype=jnp.int32)
    target_slot = targets // (2 * capacity) * capacity + targets % capacity
    hits = (slots.T[:, :, None] == target_slot).astype(f32)
    combine = jnp.sum(hits * gate_probs[:, :, None], axis=1)
    combine_high = combine.astype(bf16)
    combine_low = (combine - combine_high.astype(f32)).astype(bf16)
    both_terms = jnp.concatenate([combine_high, combine_low], axis=0)
    target_half = targets // capacity % 2
    halves = jnp.stack([jnp.where(target_half == i, both_terms, jnp.zeros((), bf16)) for i in range(2)])

    from_x = swapped(landed, "grp", 0)
    from_y = swapped(landed, "tp", 1)
    mine = (landed, from_x, from_y)
    theirs = tuple(swapped(x, "tp", 0) for x in mine)
    last_mine = swapped(from_y, "grp", 0)
    last_theirs = swapped(last_mine, "tp", 0)

    crossed = jnp.concatenate([crossed, swapped(held_until(ordered[middle:], from_y), "role", 0)], axis=0)
    arrived = lax.all_to_all(crossed, "grp", split_axis=0, concat_axis=0, tiled=True)

    blocks = jnp.stack(
        [
            (tp_rank ^ (core + 2 * y)) * 2 + (side ^ x)
            for core in range(2)
            for y, x in ((0, 0), (0, 1), (1, 0), (1, 1))
        ]
    ).astype(jnp.int32)
    gate_own, up_own = gate_weight[0].T, up_weight[0].T
    unit_count = gate_own.shape[0]
    sums = call(
        early_units,
        (shape((total_slots, unit_count), f32),) * 2,
        (blocks, *mine, *theirs, gate_own, up_own),
        smem=1,
        name="early_units",
        flops=3 * total_slots * model_width * unit_count,
    )
    sums = call(
        late_units,
        (shape((total_slots, eighth), bf16),) * 8,
        (blocks, last_mine, last_theirs, *sums, gate_own, up_own, down_weight[0], crossed),
        smem=1,
        away=1,
        name="late_units",
        flops=3 * total_slots * model_width * unit_count,
    )

    def both_cores(i):
        return sums[i].astype(f32) + swapped(sums[4 + i], "tp", 0).astype(f32)

    far = swapped(both_cores(3).astype(bf16), "grp", 0)
    sum_y = swapped((both_cores(2) + far.astype(f32)).astype(bf16), "tp", 1)
    sum_x = swapped(both_cores(1).astype(bf16), "grp", 0)
    summed = call(
        join,
        shape((total_slots, eighth), bf16),
        (sums[0], swapped(sums[4], "tp", 0), sum_x, sum_y, arrived),
        away=1,
        name="join",
    )
    returned = lax.all_to_all(
        summed.reshape(peer_count, capacity, eighth), "grp", split_axis=0, concat_axis=0, tiled=True
    ).reshape(total_slots, eighth)

    requests, max_blocks = block_table.shape
    head_dim = kv_weight.shape[2]
    draft_count = token_rows // requests
    per_kv = queries.shape[1] // head_dim
    query_rows = queries.reshape(requests, draft_count * per_kv, head_dim)
    pool = jnp.concatenate([decode_cache[:, 0], arrived], axis=0)
    stats = call(
        functools.partial(cached_attention, max_blocks=max_blocks),
        (shape((requests, draft_count * per_kv, head_dim), f32),) * 3,
        (block_table.reshape(-1), lengths, query_rows, pool),
        smem=2,
        name="cached_attention",
        flops=4 * requests * draft_count * per_kv * head_dim * max_blocks * decode_cache.shape[3],
    )
    stats = tuple(x.reshape(token_rows, per_kv * head_dim) for x in stats)
    flat_weight = kv_weight.reshape(model_width, 2 * head_dim)
    residual_out, scaled = call(
        finish,
        (shape((token_rows, quarter), f32), shape((token_rows, quarter + LANES), bf16)),
        (part, halves, returned, hidden_in, attn_gain.reshape(1, model_width), flat_weight, *stats),
        smem=1,
        away=4,
        name="finish",
    )

    scaled_core = swapped(scaled, "tp", 0)
    scaled_y = swapped(scaled, "tp", 1)
    scaled_diagonal = swapped(scaled_y, "tp", 0)
    fresh_kv, attn_out = call(
        functools.partial(last_step, draft=draft_count),
        (shape((token_rows, 2 * head_dim), bf16), shape((token_rows, per_kv * head_dim), bf16)),
        (part, scaled, scaled_core, scaled_y, scaled_diagonal, flat_weight, queries, *stats),
        smem=1,
        name="last_step",
    )
    return (residual_out, fresh_kv.reshape(token_rows, 2, head_dim), attn_out)


def solution(mesh):
    in_specs = (
        P(("role", "grp"), None),
        P(),
        P(),
        P(("role", "grp"), None),
        P("grp", None, "tp"),
        P("grp", None, "tp"),
        P("grp", "tp", None),
        P(),
        P(None, None, "tp"),
        P(("role", "grp"), "tp"),
        P(("role", "grp"), "tp", None, None, None),
        P(("role", "grp"), "tp", None, None, None),
        P(("role", "grp"), None),
        P(("role", "grp"), None),
        P(("role", "grp")),
    )
    out_specs = (P(("role", "grp"), "tp"), P(("role", "grp"), None, "tp"), P(("role", "grp"), "tp"))
    return jax.shard_map(local, mesh=mesh, in_specs=in_specs, out_specs=out_specs, check_vma=False)
```

```python
import functools

import jax
import jax.numpy as jnp
from jax import lax
from jax.experimental import pallas as pl
from jax.experimental.pallas import tpu as pltpu
from jax.sharding import PartitionSpec as P

epsilon = 1e-06
LANES = 128


def swapped(x, axis, bit):
    return lax.ppermute(x, axis, [(i, i ^ 1 << bit) for i in range(lax.axis_size(axis))])


def inverse_rms(square_sum, width):
    return lax.rsqrt(square_sum / width + epsilon)


def prepare(part_ref, routes_ref, hidden_ref, gain_ref, packed_ref, slots_ref, *, capacity):
    token_rows, model_width = hidden_ref.shape
    peers, _, eighth = packed_ref.shape
    experts = peers // 2
    quarter = 2 * eighth
    f32, bf16 = jnp.float32, jnp.bfloat16
    hidden = hidden_ref[...].astype(f32)
    squares = jnp.sum(hidden * hidden, axis=1, keepdims=True)
    columns = pl.ds(pl.multiple_of(part_ref[0] * quarter, quarter), quarter)
    own = hidden_ref[:, columns].astype(f32) * inverse_rms(squares, model_width) * gain_ref[:, columns].astype(f32)
    one_routes, two_routes = routes_ref[0:1, :], routes_ref[1:2, :]
    expert = lax.broadcasted_iota(jnp.int32, (max(experts, 8), token_rows), 0)
    one_hot, two_hot = (expert == one_routes).astype(f32), (expert == two_routes).astype(f32)
    before = lax.broadcasted_iota(jnp.int32, (token_rows, token_rows), 0) < lax.broadcasted_iota(
        jnp.int32, (token_rows, token_rows), 1
    )
    taken = jnp.dot((one_hot + two_hot).astype(bf16), before.astype(f32).astype(bf16), preferred_element_type=f32)
    one_slot = one_routes * capacity + jnp.sum(taken * one_hot, axis=0, keepdims=True).astype(jnp.int32)
    two_slot = two_routes * capacity + jnp.sum(taken * two_hot, axis=0, keepdims=True).astype(jnp.int32)
    slots_ref[0:1, :] = one_slot
    slots_ref[1:2, :] = two_slot
    target = lax.broadcasted_iota(jnp.int32, (experts * capacity, token_rows), 0)
    placing = ((target == one_slot) | (target == two_slot)).astype(f32).astype(bf16)
    packed = jnp.dot(placing, own.astype(bf16), preferred_element_type=f32)
    for e in range(experts):
        for half in range(2):
            block = packed[e * capacity : (e + 1) * capacity, half * eighth : (half + 1) * eighth]
            packed_ref[2 * e + half] = block.astype(bf16)


def wide(a, b):
    return lax.dot_general(a, b, (((1,), (1,)), ((), ())), preferred_element_type=jnp.float32)


def window(blocks_ref, i, size):
    return pl.ds(pl.multiple_of(blocks_ref[i] * size, size), size)


def early_units(blocks_ref, *refs):
    pieces, (gate_ref, up_ref, gate_out, up_out) = refs[:6], refs[6:]
    eighth = pieces[0].shape[1]
    for weight, out in ((gate_ref, gate_out), (up_ref, up_out)):
        total = None
        for i, piece in enumerate(pieces):
            more = wide(piece[...], weight[:, window(blocks_ref, 4 * (i // 3) + i % 3, eighth)])
            total = more if total is None else total + more
        out[...] = total


def late_units(blocks_ref, mine_ref, theirs_ref, gate_sum, up_sum, gate_ref, up_ref, down_ref, *refs):
    outputs = refs[-8:]
    eighth = mine_ref.shape[1]
    gate, up = gate_sum[...], up_sum[...]
    for i, piece in ((3, mine_ref), (7, theirs_ref)):
        gate = gate + wide(piece[...], gate_ref[:, window(blocks_ref, i, eighth)])
        up = up + wide(piece[...], up_ref[:, window(blocks_ref, i, eighth)])
    act = (gate / (1.0 + jnp.exp(-gate)) * up).astype(jnp.bfloat16)
    for i in (3, 7, 2, 6, 1, 5, 0, 4):
        columns = down_ref[:, window(blocks_ref, i, eighth)]
        outputs[i][...] = jnp.dot(act, columns, preferred_element_type=jnp.float32).astype(jnp.bfloat16)


def join(mine_ref, theirs_ref, x_ref, y_ref, *refs):
    total = mine_ref[...].astype(jnp.float32) + theirs_ref[...].astype(jnp.float32)
    total = total + x_ref[...].astype(jnp.float32) + y_ref[...].astype(jnp.float32)
    refs[-1][...] = total.astype(jnp.bfloat16)


def held_until(x, *others):
    def kernel(*refs):
        pass

    any_space = pl.BlockSpec(memory_space=pl.ANY)
    return pl.pallas_call(
        kernel,
        out_shape=jax.ShapeDtypeStruct(x.shape, x.dtype),
        in_specs=[any_space] * (1 + len(others)),
        out_specs=any_space,
        input_output_aliases={0: 0},
        name="held_until",
    )(x, *others)


def finish(part_ref, combine_ref, returned_ref, hidden_ref, gain_ref, *refs):
    f32, bf16 = jnp.float32, jnp.bfloat16
    residual_ref, scaled_ref = refs[-2:]
    token_rows = hidden_ref.shape[0]
    eighth = returned_ref.shape[1]
    quarter = 2 * eighth
    squares = jnp.zeros((token_rows, 1), f32)
    for half in range(2):
        start = pl.multiple_of(part_ref[0] * quarter + half * eighth, eighth)
        terms = jnp.dot(combine_ref[half], returned_ref[...], preferred_element_type=f32)
        moe = terms[:token_rows] + terms[token_rows:]
        value = hidden_ref[:, pl.ds(start, eighth)].astype(f32) + moe
        residual_ref[:, half * eighth : (half + 1) * eighth] = value
        scaled_ref[:, half * eighth : (half + 1) * eighth] = (value * gain_ref[:, pl.ds(start, eighth)].astype(f32)).astype(bf16)
        squares = squares + jnp.sum(value * value, axis=1, keepdims=True)
    high = squares.astype(bf16).astype(f32)
    lane = lax.broadcasted_iota(jnp.int32, (token_rows, LANES), 1)
    extra = jnp.where(lane == 0, high, jnp.where(lane == 1, squares - high, 0.0))
    scaled_ref[:, quarter:] = extra.astype(bf16)


def last_step(part_ref, own_ref, core_ref, y_ref, diagonal_ref, weight_ref, query_ref, top_ref, total_ref, mixed_ref, kv_ref, out_ref, *, draft):
    f32, bf16 = jnp.float32, jnp.bfloat16
    token_rows = query_ref.shape[0]
    head_dim = kv_ref.shape[1] // 2
    quarter = own_ref.shape[1] - LANES
    parts = (own_ref, core_ref, y_ref, diagonal_ref)
    squares = jnp.zeros((token_rows, LANES), f32)
    fresh = jnp.zeros((token_rows, 2 * head_dim), f32)
    for i, ref in enumerate(parts):
        rows = pl.ds(pl.multiple_of((part_ref[0] ^ i) * quarter, quarter), quarter)
        fresh = fresh + jnp.dot(ref[:, :quarter], weight_ref[rows, :], preferred_element_type=f32)
        squares = squares + ref[:, quarter:].astype(f32)
    square_sum = jnp.sum(squares, axis=1, keepdims=True)
    fresh = (fresh * inverse_rms(square_sum, len(parts) * quarter)).astype(bf16)
    kv_ref[...] = fresh
    keys = fresh[:, :head_dim]
    values = jnp.concatenate([fresh[:, head_dim:], jnp.ones((token_rows, head_dim), bf16)], axis=1)
    row = lax.broadcasted_iota(jnp.int32, (token_rows, token_rows), 0)
    col = lax.broadcasted_iota(jnp.int32, (token_rows, token_rows), 1)
    seen = (row // draft == col // draft) & (col <= row)
    for h in range(query_ref.shape[1] // head_dim):
        lanes = slice(h * head_dim, (h + 1) * head_dim)
        scores = jnp.where(seen, wide(query_ref[:, lanes], keys) * head_dim ** (-0.5), -jnp.inf)
        top = top_ref[:, lanes]
        new_top = jnp.maximum(top, jnp.max(scores, axis=1, keepdims=True))
        shrink = jnp.exp(top - new_top)
        recent = jnp.dot(jnp.exp(scores - new_top).astype(bf16), values, preferred_element_type=f32)
        denom = shrink * total_ref[:, lanes] + recent[:, head_dim:]
        out_ref[:, lanes] = ((mixed_ref[:, lanes] * shrink + recent[:, :head_dim]) / denom).astype(bf16)


def call(kernel, out_shape, args, smem=0, name=None, away=0, flops=0):
    spaces = [pltpu.SMEM] * smem + [pltpu.VMEM] * (len(args) - smem - away) + [pl.ANY] * away
    out_specs = jax.tree.map(lambda _: pl.BlockSpec(memory_space=pltpu.VMEM), out_shape)
    moved = sum(x.size * x.dtype.itemsize for x in list(args) + jax.tree.leaves(out_shape))
    return pl.pallas_call(
        kernel,
        out_shape=out_shape,
        in_specs=[pl.BlockSpec(memory_space=space) for space in spaces],
        out_specs=out_specs,
        compiler_params=pltpu.CompilerParams(vmem_limit_bytes=48 << 20),
        cost_estimate=pl.CostEstimate(flops=flops, transcendentals=0, bytes_accessed=moved),
        name=name,
    )(*args)


def cached_attention(table_ref, length_ref, query_ref, pool_ref, top_ref, total_ref, mixed_ref, *, max_blocks):
    requests, rows, head_dim = query_ref.shape
    block_len = pool_ref.shape[2]
    span = max_blocks * block_len
    scale = head_dim ** (-0.5)
    places = lax.broadcasted_iota(jnp.int32, (rows, span), 1)
    ones = jnp.ones((span, head_dim), jnp.bfloat16)

    def one(r, carry):
        ids = [table_ref[r * max_blocks + b] for b in range(max_blocks)]
        keys = jnp.concatenate([pool_ref[i, 0] for i in ids], axis=0)
        values = jnp.concatenate([pool_ref[i, 1] for i in ids], axis=0)
        values = jnp.concatenate([values, ones], axis=1)
        scores = lax.dot_general(
            query_ref[r], keys, (((1,), (1,)), ((), ())), preferred_element_type=jnp.float32
        )
        scores = jnp.where(places < length_ref[r], scores * scale, -jnp.inf)
        top = jnp.max(scores, axis=1, keepdims=True)
        exps = jnp.exp(scores - top)
        mixed = jnp.dot(exps.astype(jnp.bfloat16), values, preferred_element_type=jnp.float32)
        top_ref[r] = jnp.broadcast_to(top, (rows, head_dim))
        total_ref[r] = mixed[:, head_dim:]
        mixed_ref[r] = mixed[:, :head_dim]
        return carry

    lax.fori_loop(0, requests, one, 0, unroll=2)


def local(
    hidden_in,
    moe_gain,
    router,
    routes,
    gate_weight,
    up_weight,
    down_weight,
    attn_gain,
    kv_weight,
    queries,
    decode_cache,
    prompt_cache,
    handoff,
    block_table,
    lengths,
):
    peer_count = lax.axis_size("grp")
    expert_count = peer_count // 2
    tp_count = lax.axis_size("tp")
    tp_rank = lax.axis_index("tp")
    token_rows, model_width = hidden_in.shape
    picks_per = routes.shape[1]
    quarter = model_width // tp_count
    capacity = min(token_rows, 3 * token_rows * picks_per // (2 * expert_count))
    total_slots = 2 * expert_count * capacity
    eighth = quarter // 2
    f32, bf16 = jnp.float32, jnp.bfloat16
    shape = jax.ShapeDtypeStruct
    side = lax.axis_index("grp") & 1
    part = tp_rank.astype(jnp.int32).reshape(1)

    packed, slots = call(
        functools.partial(prepare, capacity=capacity),
        (shape((peer_count, capacity, eighth), bf16), shape((picks_per, token_rows), jnp.int32)),
        (part, routes.T, hidden_in, moe_gain.reshape(1, model_width)),
        smem=1,
        name="prepare",
    )
    landed = lax.all_to_all(packed, "grp", split_axis=0, concat_axis=0, tiled=True)
    landed = landed.reshape(total_slots, eighth)

    crossed = swapped(prompt_cache[:, 0], "role", 0)
    order = swapped(handoff, "role", 0)
    landed = held_until(landed, crossed, order)

    hidden = hidden_in.astype(f32)
    scale_in = inverse_rms(jnp.sum(hidden * hidden, axis=1, keepdims=True), model_width)
    moe_in = (hidden * scale_in * moe_gain.astype(f32)).astype(bf16)
    logits = jnp.dot(moe_in, router, preferred_element_type=f32)
    gate_probs = jax.nn.softmax(jnp.take_along_axis(logits, routes, axis=1), axis=1)
    targets = jnp.arange(total_slots, dtype=jnp.int32)
    target_slot = targets // (2 * capacity) * capacity + targets % capacity
    hits = (slots.T[:, :, None] == target_slot).astype(f32)
    combine = jnp.sum(hits * gate_probs[:, :, None], axis=1)
    combine_high = combine.astype(bf16)
    combine_low = (combine - combine_high.astype(f32)).astype(bf16)
    both_terms = jnp.concatenate([combine_high, combine_low], axis=0)
    target_half = targets // capacity % 2
    halves = jnp.stack([jnp.where(target_half == i, both_terms, jnp.zeros((), bf16)) for i in range(2)])

    from_y = swapped(landed, "tp", 1)
    from_x = held_until(swapped(landed, "grp", 0), from_y)
    mine = (landed, from_x, from_y)
    theirs = tuple(swapped(x, "tp", 0) for x in mine)
    last_mine = swapped(from_x, "tp", 1)
    last_theirs = swapped(last_mine, "tp", 0)

    ordered = held_until(crossed.at[order[0]].get(mode="promise_in_bounds"), from_x)
    arrived = lax.all_to_all(ordered, "grp", split_axis=0, concat_axis=0, tiled=True)

    blocks = jnp.stack(
        [
            (tp_rank ^ (core + 2 * y)) * 2 + (side ^ x)
            for core in range(2)
            for y, x in ((0, 0), (0, 1), (1, 0), (1, 1))
        ]
    ).astype(jnp.int32)
    gate_own, up_own = gate_weight[0].T, up_weight[0].T
    unit_count = gate_own.shape[0]
    sums = call(
        early_units,
        (shape((total_slots, unit_count), f32),) * 2,
        (blocks, *mine, *theirs, gate_own, up_own),
        smem=1,
        name="early_units",
        flops=3 * total_slots * model_width * unit_count,
    )
    sums = call(
        late_units,
        (shape((total_slots, eighth), bf16),) * 8,
        (blocks, last_mine, last_theirs, *sums, gate_own, up_own, down_weight[0], ordered),
        smem=1,
        away=1,
        name="late_units",
        flops=3 * total_slots * model_width * unit_count,
    )

    requests, max_blocks = block_table.shape
    head_dim = kv_weight.shape[2]
    draft_count = token_rows // requests
    per_kv = queries.shape[1] // head_dim
    query_rows = queries.reshape(requests, draft_count * per_kv, head_dim)
    pool = jnp.concatenate([decode_cache[:, 0], arrived], axis=0)
    stats = call(
        functools.partial(cached_attention, max_blocks=max_blocks),
        (shape((requests, draft_count * per_kv, head_dim), f32),) * 3,
        (block_table.reshape(-1), lengths, query_rows, pool),
        smem=2,
        name="cached_attention",
        flops=4 * requests * draft_count * per_kv * head_dim * max_blocks * decode_cache.shape[3],
    )

    def both_cores(i):
        return sums[i].astype(f32) + swapped(sums[4 + i], "tp", 0).astype(f32)

    far = swapped(both_cores(3).astype(bf16), "tp", 1)
    sum_x = swapped((both_cores(1) + far.astype(f32)).astype(bf16), "grp", 0)
    sum_y = swapped(held_until(both_cores(2).astype(bf16), far), "tp", 1)
    summed = call(
        join,
        shape((total_slots, eighth), bf16),
        (sums[0], swapped(sums[4], "tp", 0), sum_x, sum_y, *stats),
        away=3,
        name="join",
    )
    returned = lax.all_to_all(
        summed.reshape(peer_count, capacity, eighth), "grp", split_axis=0, concat_axis=0, tiled=True
    ).reshape(total_slots, eighth)
    stats = tuple(x.reshape(token_rows, per_kv * head_dim) for x in stats)
    flat_weight = kv_weight.reshape(model_width, 2 * head_dim)
    residual_out, scaled = call(
        finish,
        (shape((token_rows, quarter), f32), shape((token_rows, quarter + LANES), bf16)),
        (part, halves, returned, hidden_in, attn_gain.reshape(1, model_width), flat_weight, *stats),
        smem=1,
        away=4,
        name="finish",
    )

    scaled_core = swapped(scaled, "tp", 0)
    scaled_y = swapped(scaled, "tp", 1)
    scaled_diagonal = swapped(scaled_y, "tp", 0)
    fresh_kv, attn_out = call(
        functools.partial(last_step, draft=draft_count),
        (shape((token_rows, 2 * head_dim), bf16), shape((token_rows, per_kv * head_dim), bf16)),
        (part, scaled, scaled_core, scaled_y, scaled_diagonal, flat_weight, queries, *stats),
        smem=1,
        name="last_step",
    )
    return (residual_out, fresh_kv.reshape(token_rows, 2, head_dim), attn_out)


def solution(mesh):
    in_specs = (
        P(("role", "grp"), None),
        P(),
        P(),
        P(("role", "grp"), None),
        P("grp", None, "tp"),
        P("grp", None, "tp"),
        P("grp", "tp", None),
        P(),
        P(None, None, "tp"),
        P(("role", "grp"), "tp"),
        P(("role", "grp"), "tp", None, None, None),
        P(("role", "grp"), "tp", None, None, None),
        P(("role", "grp"), None),
        P(("role", "grp"), None),
        P(("role", "grp")),
    )
    out_specs = (P(("role", "grp"), "tp"), P(("role", "grp"), None, "tp"), P(("role", "grp"), "tp"))
    return jax.shard_map(local, mesh=mesh, in_specs=in_specs, out_specs=out_specs, check_vma=False)
```

```python
import functools

import jax
import jax.numpy as jnp
from jax import lax
from jax.experimental import pallas as pl
from jax.experimental.pallas import tpu as pltpu
from jax.sharding import PartitionSpec as P

epsilon = 1e-06
LANES = 128


def swapped(x, axis, bit):
    return lax.ppermute(x, axis, [(i, i ^ 1 << bit) for i in range(lax.axis_size(axis))])


def inverse_rms(square_sum, width):
    return lax.rsqrt(square_sum / width + epsilon)


def prepare(part_ref, routes_ref, hidden_ref, gain_ref, packed_ref, slots_ref, scale_ref, *, capacity):
    token_rows, model_width = hidden_ref.shape
    peers, _, eighth = packed_ref.shape
    experts = peers // 2
    quarter = 2 * eighth
    f32, bf16 = jnp.float32, jnp.bfloat16
    hidden = hidden_ref[...].astype(f32)
    squares = jnp.sum(hidden * hidden, axis=1, keepdims=True)
    columns = pl.ds(pl.multiple_of(part_ref[0] * quarter, quarter), quarter)
    scale = inverse_rms(squares, model_width)
    scale_ref[...] = jnp.broadcast_to(scale, scale_ref.shape)
    own = hidden_ref[:, columns].astype(f32) * scale * gain_ref[:, columns].astype(f32)
    one_routes, two_routes = routes_ref[0:1, :], routes_ref[1:2, :]
    expert = lax.broadcasted_iota(jnp.int32, (max(experts, 8), token_rows), 0)
    one_hot, two_hot = (expert == one_routes).astype(f32), (expert == two_routes).astype(f32)
    before = lax.broadcasted_iota(jnp.int32, (token_rows, token_rows), 0) < lax.broadcasted_iota(
        jnp.int32, (token_rows, token_rows), 1
    )
    taken = jnp.dot((one_hot + two_hot).astype(bf16), before.astype(f32).astype(bf16), preferred_element_type=f32)
    one_slot = one_routes * capacity + jnp.sum(taken * one_hot, axis=0, keepdims=True).astype(jnp.int32)
    two_slot = two_routes * capacity + jnp.sum(taken * two_hot, axis=0, keepdims=True).astype(jnp.int32)
    slots_ref[0:1, :] = one_slot
    slots_ref[1:2, :] = two_slot
    target = lax.broadcasted_iota(jnp.int32, (experts * capacity, token_rows), 0)
    placing = ((target == one_slot) | (target == two_slot)).astype(f32).astype(bf16)
    packed = jnp.dot(placing, own.astype(bf16), preferred_element_type=f32)
    for e in range(experts):
        for half in range(2):
            block = packed[e * capacity : (e + 1) * capacity, half * eighth : (half + 1) * eighth]
            packed_ref[2 * e + half] = block.astype(bf16)


def wide(a, b):
    return lax.dot_general(a, b, (((1,), (1,)), ((), ())), preferred_element_type=jnp.float32)


def window(blocks_ref, i, size):
    return pl.ds(pl.multiple_of(blocks_ref[i] * size, size), size)


def early_units(blocks_ref, *refs):
    pieces, (gate_ref, up_ref, gate_out, up_out) = refs[:6], refs[6:]
    eighth = pieces[0].shape[1]
    for weight, out in ((gate_ref, gate_out), (up_ref, up_out)):
        total = None
        for i, piece in enumerate(pieces):
            more = wide(piece[...], weight[:, window(blocks_ref, 4 * (i // 3) + i % 3, eighth)])
            total = more if total is None else total + more
        out[...] = total


def late_units(blocks_ref, mine_low, mine_high, theirs_low, theirs_high, gate_sum, up_sum, gate_ref, up_ref, down_ref, *refs):
    outputs = refs[-8:]
    eighth = mine_low.shape[1]
    gate, up = gate_sum[...], up_sum[...]
    for i, low, high in ((3, mine_low, mine_high), (7, theirs_low, theirs_high)):
        piece = jnp.concatenate([low[...], high[...]], axis=0)
        gate = gate + wide(piece, gate_ref[:, window(blocks_ref, i, eighth)])
        up = up + wide(piece, up_ref[:, window(blocks_ref, i, eighth)])
    act = (gate / (1.0 + jnp.exp(-gate)) * up).astype(jnp.bfloat16)
    for i in (3, 7, 2, 6, 1, 5, 0, 4):
        columns = down_ref[:, window(blocks_ref, i, eighth)]
        outputs[i][...] = jnp.dot(act, columns, preferred_element_type=jnp.float32).astype(jnp.bfloat16)


def turn(mine_x, theirs_x, mine_y, theirs_y, low_ref, high_ref, x_ref, y_ref):
    half = low_ref.shape[0]
    for mine, theirs, far, part, out in ((mine_x, theirs_x, low_ref, 0, x_ref), (mine_y, theirs_y, high_ref, 1, y_ref)):
        for i in range(2):
            span = slice(i * half, (i + 1) * half)
            total = mine[span].astype(jnp.float32) + theirs[span].astype(jnp.float32)
            if i == part:
                total = total + far[...].astype(jnp.float32)
            out[span] = total.astype(jnp.bfloat16)


def join(mine_ref, theirs_ref, x_ref, y_ref, *refs):
    total = mine_ref[...].astype(jnp.float32) + theirs_ref[...].astype(jnp.float32)
    total = total + x_ref[...].astype(jnp.float32) + y_ref[...].astype(jnp.float32)
    refs[-1][...] = total.astype(jnp.bfloat16)


def held_until(x, *others):
    def kernel(*refs):
        pass

    any_space = pl.BlockSpec(memory_space=pl.ANY)
    return pl.pallas_call(
        kernel,
        out_shape=jax.ShapeDtypeStruct(x.shape, x.dtype),
        in_specs=[any_space] * (1 + len(others)),
        out_specs=any_space,
        input_output_aliases={0: 0},
        name="held_until",
    )(x, *others)


def finish(part_ref, combine_ref, returned_ref, hidden_ref, gain_ref, *refs):
    f32, bf16 = jnp.float32, jnp.bfloat16
    residual_ref, scaled_ref = refs[-2:]
    token_rows = hidden_ref.shape[0]
    eighth = returned_ref.shape[1]
    quarter = 2 * eighth
    squares = jnp.zeros((token_rows, 1), f32)
    for half in range(2):
        start = pl.multiple_of(part_ref[0] * quarter + half * eighth, eighth)
        terms = jnp.dot(combine_ref[half], returned_ref[...], preferred_element_type=f32)
        moe = terms[:token_rows] + terms[token_rows:]
        value = hidden_ref[:, pl.ds(start, eighth)].astype(f32) + moe
        residual_ref[:, half * eighth : (half + 1) * eighth] = value
        scaled_ref[:, half * eighth : (half + 1) * eighth] = (value * gain_ref[:, pl.ds(start, eighth)].astype(f32)).astype(bf16)
        squares = squares + jnp.sum(value * value, axis=1, keepdims=True)
    high = squares.astype(bf16).astype(f32)
    lane = lax.broadcasted_iota(jnp.int32, (token_rows, LANES), 1)
    extra = jnp.where(lane == 0, high, jnp.where(lane == 1, squares - high, 0.0))
    scaled_ref[:, quarter:] = extra.astype(bf16)


def last_step(part_ref, own_ref, core_ref, y_ref, diagonal_ref, weight_ref, query_ref, top_ref, total_ref, mixed_ref, kv_ref, out_ref, *, draft):
    f32, bf16 = jnp.float32, jnp.bfloat16
    token_rows = query_ref.shape[0]
    head_dim = kv_ref.shape[1] // 2
    quarter = own_ref.shape[1] - LANES
    parts = (own_ref, core_ref, y_ref, diagonal_ref)
    squares = jnp.zeros((token_rows, LANES), f32)
    fresh = jnp.zeros((token_rows, 2 * head_dim), f32)
    for i, ref in enumerate(parts):
        rows = pl.ds(pl.multiple_of((part_ref[0] ^ i) * quarter, quarter), quarter)
        fresh = fresh + jnp.dot(ref[:, :quarter], weight_ref[rows, :], preferred_element_type=f32)
        squares = squares + ref[:, quarter:].astype(f32)
    square_sum = jnp.sum(squares, axis=1, keepdims=True)
    fresh = (fresh * inverse_rms(square_sum, len(parts) * quarter)).astype(bf16)
    kv_ref[...] = fresh
    keys = fresh[:, :head_dim]
    values = jnp.concatenate([fresh[:, head_dim:], jnp.ones((token_rows, head_dim), bf16)], axis=1)
    row = lax.broadcasted_iota(jnp.int32, (token_rows, token_rows), 0)
    col = lax.broadcasted_iota(jnp.int32, (token_rows, token_rows), 1)
    seen = (row // draft == col // draft) & (col <= row)
    for h in range(query_ref.shape[1] // head_dim):
        lanes = slice(h * head_dim, (h + 1) * head_dim)
        scores = jnp.where(seen, wide(query_ref[:, lanes], keys) * head_dim ** (-0.5), -jnp.inf)
        top = top_ref[:, lanes]
        new_top = jnp.maximum(top, jnp.max(scores, axis=1, keepdims=True))
        shrink = jnp.exp(top - new_top)
        recent = jnp.dot(jnp.exp(scores - new_top).astype(bf16), values, preferred_element_type=f32)
        denom = shrink * total_ref[:, lanes] + recent[:, head_dim:]
        out_ref[:, lanes] = ((mixed_ref[:, lanes] * shrink + recent[:, :head_dim]) / denom).astype(bf16)


def call(kernel, out_shape, args, smem=0, name=None, away=0, flops=0):
    spaces = [pltpu.SMEM] * smem + [pltpu.VMEM] * (len(args) - smem - away) + [pl.ANY] * away
    out_specs = jax.tree.map(lambda _: pl.BlockSpec(memory_space=pltpu.VMEM), out_shape)
    moved = sum(x.size * x.dtype.itemsize for x in list(args) + jax.tree.leaves(out_shape))
    return pl.pallas_call(
        kernel,
        out_shape=out_shape,
        in_specs=[pl.BlockSpec(memory_space=space) for space in spaces],
        out_specs=out_specs,
        compiler_params=pltpu.CompilerParams(vmem_limit_bytes=48 << 20),
        cost_estimate=pl.CostEstimate(flops=flops, transcendentals=0, bytes_accessed=moved),
        name=name,
    )(*args)


def cached_attention(table_ref, length_ref, query_ref, pool_ref, top_ref, total_ref, mixed_ref, *, max_blocks):
    requests, rows, head_dim = query_ref.shape
    block_len = pool_ref.shape[2]
    span = max_blocks * block_len
    scale = head_dim ** (-0.5)
    places = lax.broadcasted_iota(jnp.int32, (rows, span), 1)
    ones = jnp.ones((span, head_dim), jnp.bfloat16)

    def one(r, carry):
        ids = [table_ref[r * max_blocks + b] for b in range(max_blocks)]
        keys = jnp.concatenate([pool_ref[i, 0] for i in ids], axis=0)
        values = jnp.concatenate([pool_ref[i, 1] for i in ids], axis=0)
        values = jnp.concatenate([values, ones], axis=1)
        scores = lax.dot_general(
            query_ref[r], keys, (((1,), (1,)), ((), ())), preferred_element_type=jnp.float32
        )
        scores = jnp.where(places < length_ref[r], scores * scale, -jnp.inf)
        top = jnp.max(scores, axis=1, keepdims=True)
        exps = jnp.exp(scores - top)
        mixed = jnp.dot(exps.astype(jnp.bfloat16), values, preferred_element_type=jnp.float32)
        top_ref[r] = jnp.broadcast_to(top, (rows, head_dim))
        total_ref[r] = mixed[:, head_dim:]
        mixed_ref[r] = mixed[:, :head_dim]
        return carry

    lax.fori_loop(0, requests, one, 0, unroll=2)


def local(
    hidden_in,
    moe_gain,
    router,
    routes,
    gate_weight,
    up_weight,
    down_weight,
    attn_gain,
    kv_weight,
    queries,
    decode_cache,
    prompt_cache,
    handoff,
    block_table,
    lengths,
):
    peer_count = lax.axis_size("grp")
    expert_count = peer_count // 2
    tp_count = lax.axis_size("tp")
    tp_rank = lax.axis_index("tp")
    token_rows, model_width = hidden_in.shape
    picks_per = routes.shape[1]
    quarter = model_width // tp_count
    capacity = min(token_rows, 3 * token_rows * picks_per // (2 * expert_count))
    total_slots = 2 * expert_count * capacity
    eighth = quarter // 2
    f32, bf16 = jnp.float32, jnp.bfloat16
    shape = jax.ShapeDtypeStruct
    side = lax.axis_index("grp") & 1
    part = tp_rank.astype(jnp.int32).reshape(1)

    packed, slots, scale_in = call(
        functools.partial(prepare, capacity=capacity),
        (shape((peer_count, capacity, eighth), bf16), shape((picks_per, token_rows), jnp.int32), shape((token_rows, LANES), f32)),
        (part, routes.T, hidden_in, moe_gain.reshape(1, model_width)),
        smem=1,
        name="prepare",
    )
    landed = lax.all_to_all(packed, "grp", split_axis=0, concat_axis=0, tiled=True)
    landed = landed.reshape(total_slots, eighth)

    crossed = swapped(prompt_cache[:, 0], "role", 0)
    order = swapped(handoff, "role", 0)

    hidden = hidden_in.astype(f32)
    moe_in = (hidden * scale_in[:, :1] * moe_gain.astype(f32)).astype(bf16)
    logits = jnp.dot(moe_in, router, preferred_element_type=f32)
    gate_probs = jax.nn.softmax(jnp.take_along_axis(logits, routes, axis=1), axis=1)
    targets = jnp.arange(total_slots, dtype=jnp.int32)
    target_slot = targets // (2 * capacity) * capacity + targets % capacity
    hits = (slots.T[:, :, None] == target_slot).astype(f32)
    combine = jnp.sum(hits * gate_probs[:, :, None], axis=1)
    combine_high = combine.astype(bf16)
    combine_low = (combine - combine_high.astype(f32)).astype(bf16)
    both_terms = jnp.concatenate([combine_high, combine_low], axis=0)
    target_half = targets // capacity % 2
    halves = jnp.stack([jnp.where(target_half == i, both_terms, jnp.zeros((), bf16)) for i in range(2)])

    requests, max_blocks = block_table.shape
    head_dim = kv_weight.shape[2]
    flat_weight = kv_weight.reshape(model_width, 2 * head_dim)
    middle = total_slots // 2
    landed = held_until(landed, crossed, order, halves, flat_weight)
    from_y = swapped(landed, "tp", 1)
    from_x = held_until(swapped(landed, "grp", 0), from_y)
    landed_core = swapped(landed, "tp", 0)
    mine = (landed, from_x, from_y)
    theirs = (landed_core, swapped(from_x, "tp", 0), swapped(from_y, "tp", 0))
    last_mine = (swapped(from_x[:middle], "tp", 1), swapped(from_y[middle:], "grp", 0))
    last_theirs = tuple(swapped(x, "tp", 0) for x in last_mine)

    order = held_until(order, landed_core)
    ordered = crossed.at[order[0]].get(mode="promise_in_bounds")
    arrived = lax.all_to_all(ordered, "grp", split_axis=0, concat_axis=0, tiled=True)

    blocks = jnp.stack(
        [
            (tp_rank ^ (core + 2 * y)) * 2 + (side ^ x)
            for core in range(2)
            for y, x in ((0, 0), (0, 1), (1, 0), (1, 1))
        ]
    ).astype(jnp.int32)
    gate_own, up_own = gate_weight[0].T, up_weight[0].T
    unit_count = gate_own.shape[0]
    sums = call(
        early_units,
        (shape((total_slots, unit_count), f32),) * 2,
        (blocks, *mine, *theirs, gate_own, up_own),
        smem=1,
        name="early_units",
        flops=3 * total_slots * model_width * unit_count,
    )
    sums = call(
        late_units,
        (shape((total_slots, eighth), bf16),) * 8,
        (blocks, *last_mine, *last_theirs, *sums, gate_own, up_own, down_weight[0], ordered),
        smem=1,
        away=1,
        name="late_units",
        flops=3 * total_slots * model_width * unit_count,
    )

    draft_count = token_rows // requests
    per_kv = queries.shape[1] // head_dim
    query_rows = queries.reshape(requests, draft_count * per_kv, head_dim)
    pool = jnp.concatenate([decode_cache[:, 0], arrived], axis=0)
    stats = call(
        functools.partial(cached_attention, max_blocks=max_blocks),
        (shape((requests, draft_count * per_kv, head_dim), f32),) * 3,
        (block_table.reshape(-1), lengths, query_rows, pool),
        smem=2,
        name="cached_attention",
        flops=4 * requests * draft_count * per_kv * head_dim * max_blocks * decode_cache.shape[3],
    )

    from_core = tuple(swapped(x, "tp", 0) for x in sums[4:])
    both_ways = (sums[3].astype(f32) + from_core[3].astype(f32)).astype(bf16)
    low, high = swapped(both_ways[:middle], "tp", 1), swapped(both_ways[middle:], "grp", 0)
    to_x, to_y = call(
        turn,
        (shape((total_slots, eighth), bf16),) * 2,
        (sums[1], from_core[1], sums[2], from_core[2], low, high),
        name="turn",
    )
    sum_x, sum_y = swapped(to_x, "grp", 0), swapped(to_y, "tp", 1)
    summed = call(
        join,
        shape((total_slots, eighth), bf16),
        (sums[0], from_core[0], sum_x, sum_y, *stats),
        away=3,
        name="join",
    )
    returned = lax.all_to_all(
        summed.reshape(peer_count, capacity, eighth), "grp", split_axis=0, concat_axis=0, tiled=True
    ).reshape(total_slots, eighth)
    stats = tuple(x.reshape(token_rows, per_kv * head_dim) for x in stats)
    residual_out, scaled = call(
        finish,
        (shape((token_rows, quarter), f32), shape((token_rows, quarter + LANES), bf16)),
        (part, halves, returned, hidden_in, attn_gain.reshape(1, model_width), *stats),
        smem=1,
        away=3,
        name="finish",
    )

    scaled_core = swapped(scaled, "tp", 0)
    scaled_y = swapped(scaled, "tp", 1)
    scaled_diagonal = swapped(scaled_y, "tp", 0)
    fresh_kv, attn_out = call(
        functools.partial(last_step, draft=draft_count),
        (shape((token_rows, 2 * head_dim), bf16), shape((token_rows, per_kv * head_dim), bf16)),
        (part, scaled, scaled_core, scaled_y, scaled_diagonal, flat_weight, queries, *stats),
        smem=1,
        name="last_step",
    )
    return (residual_out, fresh_kv.reshape(token_rows, 2, head_dim), attn_out)


def solution(mesh):
    in_specs = (
        P(("role", "grp"), None),
        P(),
        P(),
        P(("role", "grp"), None),
        P("grp", None, "tp"),
        P("grp", None, "tp"),
        P("grp", "tp", None),
        P(),
        P(None, None, "tp"),
        P(("role", "grp"), "tp"),
        P(("role", "grp"), "tp", None, None, None),
        P(("role", "grp"), "tp", None, None, None),
        P(("role", "grp"), None),
        P(("role", "grp"), None),
        P(("role", "grp")),
    )
    out_specs = (P(("role", "grp"), "tp"), P(("role", "grp"), None, "tp"), P(("role", "grp"), "tp"))
    return jax.shard_map(local, mesh=mesh, in_specs=in_specs, out_specs=out_specs, check_vma=False)
```

```python
import functools

import jax
import jax.numpy as jnp
from jax import lax
from jax.experimental import pallas as pl
from jax.experimental.pallas import tpu as pltpu
from jax.sharding import PartitionSpec as P

epsilon = 1e-06
LANES = 128


def swapped(x, axis, bit):
    return lax.ppermute(x, axis, [(i, i ^ 1 << bit) for i in range(lax.axis_size(axis))])


def inverse_rms(square_sum, width):
    return lax.rsqrt(square_sum / width + epsilon)


def prepare(part_ref, routes_ref, hidden_ref, gain_ref, packed_ref, slots_ref, scale_ref, *, capacity):
    token_rows, model_width = hidden_ref.shape
    peers, _, eighth = packed_ref.shape
    experts = peers // 2
    quarter = 2 * eighth
    f32, bf16 = jnp.float32, jnp.bfloat16
    hidden = hidden_ref[...].astype(f32)
    squares = jnp.sum(hidden * hidden, axis=1, keepdims=True)
    columns = pl.ds(pl.multiple_of(part_ref[0] * quarter, quarter), quarter)
    scale = inverse_rms(squares, model_width)
    scale_ref[...] = jnp.broadcast_to(scale, scale_ref.shape)
    own = hidden_ref[:, columns].astype(f32) * scale * gain_ref[:, columns].astype(f32)
    one_routes, two_routes = routes_ref[0:1, :], routes_ref[1:2, :]
    expert = lax.broadcasted_iota(jnp.int32, (max(experts, 8), token_rows), 0)
    one_hot, two_hot = (expert == one_routes).astype(f32), (expert == two_routes).astype(f32)
    before = lax.broadcasted_iota(jnp.int32, (token_rows, token_rows), 0) < lax.broadcasted_iota(
        jnp.int32, (token_rows, token_rows), 1
    )
    taken = jnp.dot((one_hot + two_hot).astype(bf16), before.astype(f32).astype(bf16), preferred_element_type=f32)
    one_slot = one_routes * capacity + jnp.sum(taken * one_hot, axis=0, keepdims=True).astype(jnp.int32)
    two_slot = two_routes * capacity + jnp.sum(taken * two_hot, axis=0, keepdims=True).astype(jnp.int32)
    slots_ref[0:1, :] = one_slot
    slots_ref[1:2, :] = two_slot
    target = lax.broadcasted_iota(jnp.int32, (experts * capacity, token_rows), 0)
    placing = ((target == one_slot) | (target == two_slot)).astype(f32).astype(bf16)
    packed = jnp.dot(placing, own.astype(bf16), preferred_element_type=f32)
    for e in range(experts):
        for half in range(2):
            block = packed[e * capacity : (e + 1) * capacity, half * eighth : (half + 1) * eighth]
            packed_ref[2 * e + half] = block.astype(bf16)


def wide(a, b):
    return lax.dot_general(a, b, (((1,), (1,)), ((), ())), preferred_element_type=jnp.float32)


def window(blocks_ref, i, size):
    return pl.ds(pl.multiple_of(blocks_ref[i] * size, size), size)


def early_units(blocks_ref, *refs):
    pieces, (gate_ref, up_ref, gate_out, up_out) = refs[:6], refs[6:]
    eighth = pieces[0].shape[1]
    for weight, out in ((gate_ref, gate_out), (up_ref, up_out)):
        total = None
        for i, piece in enumerate(pieces):
            more = wide(piece[...], weight[:, window(blocks_ref, 4 * (i // 3) + i % 3, eighth)])
            total = more if total is None else total + more
        out[...] = total


def late_units(blocks_ref, mine_low, mine_high, theirs_low, theirs_high, gate_sum, up_sum, gate_ref, up_ref, down_ref, *refs):
    outputs = refs[-8:]
    eighth = mine_low.shape[1]
    gate, up = gate_sum[...], up_sum[...]
    for i, low, high in ((3, mine_low, mine_high), (7, theirs_low, theirs_high)):
        piece = jnp.concatenate([low[...], high[...]], axis=0)
        gate = gate + wide(piece, gate_ref[:, window(blocks_ref, i, eighth)])
        up = up + wide(piece, up_ref[:, window(blocks_ref, i, eighth)])
    act = (gate / (1.0 + jnp.exp(-gate)) * up).astype(jnp.bfloat16)
    for i in (3, 7, 2, 6, 1, 5, 0, 4):
        columns = down_ref[:, window(blocks_ref, i, eighth)]
        outputs[i][...] = jnp.dot(act, columns, preferred_element_type=jnp.float32).astype(jnp.bfloat16)


def turn(mine_x, theirs_x, mine_y, theirs_y, low_ref, high_ref, *refs):
    x_ref, y_ref = refs[-2:]
    half = low_ref.shape[0]
    for mine, theirs, far, part, out in ((mine_x, theirs_x, low_ref, 0, x_ref), (mine_y, theirs_y, high_ref, 1, y_ref)):
        for i in range(2):
            span = slice(i * half, (i + 1) * half)
            total = mine[span].astype(jnp.float32) + theirs[span].astype(jnp.float32)
            if i == part:
                total = total + far[...].astype(jnp.float32)
            out[span] = total.astype(jnp.bfloat16)


def join(mine_ref, theirs_ref, x_ref, y_ref, *refs):
    total = mine_ref[...].astype(jnp.float32) + theirs_ref[...].astype(jnp.float32)
    total = total + x_ref[...].astype(jnp.float32) + y_ref[...].astype(jnp.float32)
    refs[-1][...] = total.astype(jnp.bfloat16)


def held_until(x, *others):
    def kernel(*refs):
        pass

    any_space = pl.BlockSpec(memory_space=pl.ANY)
    return pl.pallas_call(
        kernel,
        out_shape=jax.ShapeDtypeStruct(x.shape, x.dtype),
        in_specs=[any_space] * (1 + len(others)),
        out_specs=any_space,
        input_output_aliases={0: 0},
        name="held_until",
    )(x, *others)


def finish(part_ref, combine_ref, returned_ref, hidden_ref, gain_ref, *refs):
    f32, bf16 = jnp.float32, jnp.bfloat16
    residual_ref, scaled_ref = refs[-2:]
    token_rows = hidden_ref.shape[0]
    eighth = returned_ref.shape[1]
    quarter = 2 * eighth
    squares = jnp.zeros((token_rows, 1), f32)
    for half in range(2):
        start = pl.multiple_of(part_ref[0] * quarter + half * eighth, eighth)
        terms = jnp.dot(combine_ref[half], returned_ref[...], preferred_element_type=f32)
        moe = terms[:token_rows] + terms[token_rows:]
        value = hidden_ref[:, pl.ds(start, eighth)].astype(f32) + moe
        residual_ref[:, half * eighth : (half + 1) * eighth] = value
        scaled_ref[:, half * eighth : (half + 1) * eighth] = (value * gain_ref[:, pl.ds(start, eighth)].astype(f32)).astype(bf16)
        squares = squares + jnp.sum(value * value, axis=1, keepdims=True)
    high = squares.astype(bf16).astype(f32)
    lane = lax.broadcasted_iota(jnp.int32, (token_rows, LANES), 1)
    extra = jnp.where(lane == 0, high, jnp.where(lane == 1, squares - high, 0.0))
    scaled_ref[:, quarter:] = extra.astype(bf16)


def last_step(part_ref, own_ref, core_ref, y_ref, diagonal_ref, weight_ref, query_ref, top_ref, total_ref, mixed_ref, kv_ref, out_ref, *, draft):
    f32, bf16 = jnp.float32, jnp.bfloat16
    token_rows = query_ref.shape[0]
    head_dim = kv_ref.shape[1] // 2
    quarter = own_ref.shape[1] - LANES
    parts = (own_ref, core_ref, y_ref, diagonal_ref)
    squares = jnp.zeros((token_rows, LANES), f32)
    fresh = jnp.zeros((token_rows, 2 * head_dim), f32)
    for i, ref in enumerate(parts):
        rows = pl.ds(pl.multiple_of((part_ref[0] ^ i) * quarter, quarter), quarter)
        fresh = fresh + jnp.dot(ref[:, :quarter], weight_ref[rows, :], preferred_element_type=f32)
        squares = squares + ref[:, quarter:].astype(f32)
    square_sum = jnp.sum(squares, axis=1, keepdims=True)
    fresh = (fresh * inverse_rms(square_sum, len(parts) * quarter)).astype(bf16)
    kv_ref[...] = fresh
    keys = fresh[:, :head_dim]
    values = jnp.concatenate([fresh[:, head_dim:], jnp.ones((token_rows, head_dim), bf16)], axis=1)
    row = lax.broadcasted_iota(jnp.int32, (token_rows, token_rows), 0)
    col = lax.broadcasted_iota(jnp.int32, (token_rows, token_rows), 1)
    seen = (row // draft == col // draft) & (col <= row)
    for h in range(query_ref.shape[1] // head_dim):
        lanes = slice(h * head_dim, (h + 1) * head_dim)
        scores = jnp.where(seen, wide(query_ref[:, lanes], keys) * head_dim ** (-0.5), -jnp.inf)
        top = top_ref[:, lanes]
        new_top = jnp.maximum(top, jnp.max(scores, axis=1, keepdims=True))
        shrink = jnp.exp(top - new_top)
        recent = jnp.dot(jnp.exp(scores - new_top).astype(bf16), values, preferred_element_type=f32)
        denom = shrink * total_ref[:, lanes] + recent[:, head_dim:]
        out_ref[:, lanes] = ((mixed_ref[:, lanes] * shrink + recent[:, :head_dim]) / denom).astype(bf16)


def call(kernel, out_shape, args, smem=0, name=None, away=0, flops=0):
    spaces = [pltpu.SMEM] * smem + [pltpu.VMEM] * (len(args) - smem - away) + [pl.ANY] * away
    out_specs = jax.tree.map(lambda _: pl.BlockSpec(memory_space=pltpu.VMEM), out_shape)
    moved = sum(x.size * x.dtype.itemsize for x in list(args) + jax.tree.leaves(out_shape))
    return pl.pallas_call(
        kernel,
        out_shape=out_shape,
        in_specs=[pl.BlockSpec(memory_space=space) for space in spaces],
        out_specs=out_specs,
        compiler_params=pltpu.CompilerParams(vmem_limit_bytes=48 << 20),
        cost_estimate=pl.CostEstimate(flops=flops, transcendentals=0, bytes_accessed=moved),
        name=name,
    )(*args)


def cached_attention(table_ref, length_ref, query_ref, pool_ref, top_ref, total_ref, mixed_ref, *, max_blocks):
    requests, rows, head_dim = query_ref.shape
    block_len = pool_ref.shape[2]
    span = max_blocks * block_len
    scale = head_dim ** (-0.5)
    places = lax.broadcasted_iota(jnp.int32, (rows, span), 1)
    ones = jnp.ones((span, head_dim), jnp.bfloat16)

    def one(r, carry):
        ids = [table_ref[r * max_blocks + b] for b in range(max_blocks)]
        keys = jnp.concatenate([pool_ref[i, 0] for i in ids], axis=0)
        values = jnp.concatenate([pool_ref[i, 1] for i in ids], axis=0)
        values = jnp.concatenate([values, ones], axis=1)
        scores = lax.dot_general(
            query_ref[r], keys, (((1,), (1,)), ((), ())), preferred_element_type=jnp.float32
        )
        scores = jnp.where(places < length_ref[r], scores * scale, -jnp.inf)
        top = jnp.max(scores, axis=1, keepdims=True)
        exps = jnp.exp(scores - top)
        mixed = jnp.dot(exps.astype(jnp.bfloat16), values, preferred_element_type=jnp.float32)
        top_ref[r] = jnp.broadcast_to(top, (rows, head_dim))
        total_ref[r] = mixed[:, head_dim:]
        mixed_ref[r] = mixed[:, :head_dim]
        return carry

    lax.fori_loop(0, requests, one, 0, unroll=2)


def local(
    hidden_in,
    moe_gain,
    router,
    routes,
    gate_weight,
    up_weight,
    down_weight,
    attn_gain,
    kv_weight,
    queries,
    decode_cache,
    prompt_cache,
    handoff,
    block_table,
    lengths,
):
    peer_count = lax.axis_size("grp")
    expert_count = peer_count // 2
    tp_count = lax.axis_size("tp")
    tp_rank = lax.axis_index("tp")
    token_rows, model_width = hidden_in.shape
    picks_per = routes.shape[1]
    quarter = model_width // tp_count
    capacity = min(token_rows, 3 * token_rows * picks_per // (2 * expert_count))
    total_slots = 2 * expert_count * capacity
    eighth = quarter // 2
    f32, bf16 = jnp.float32, jnp.bfloat16
    shape = jax.ShapeDtypeStruct
    side = lax.axis_index("grp") & 1
    part = tp_rank.astype(jnp.int32).reshape(1)

    packed, slots, scale_in = call(
        functools.partial(prepare, capacity=capacity),
        (shape((peer_count, capacity, eighth), bf16), shape((picks_per, token_rows), jnp.int32), shape((token_rows, LANES), f32)),
        (part, routes.T, hidden_in, moe_gain.reshape(1, model_width)),
        smem=1,
        name="prepare",
    )
    landed = lax.all_to_all(packed, "grp", split_axis=0, concat_axis=0, tiled=True)
    landed = landed.reshape(total_slots, eighth)

    crossed = swapped(prompt_cache[:, 0], "role", 0)
    order = swapped(handoff, "role", 0)

    hidden = hidden_in.astype(f32)
    moe_in = (hidden * scale_in[:, :1] * moe_gain.astype(f32)).astype(bf16)
    logits = jnp.dot(moe_in, router, preferred_element_type=f32)
    gate_probs = jax.nn.softmax(jnp.take_along_axis(logits, routes, axis=1), axis=1)
    targets = jnp.arange(total_slots, dtype=jnp.int32)
    target_slot = targets // (2 * capacity) * capacity + targets % capacity
    hits = (slots.T[:, :, None] == target_slot).astype(f32)
    combine = jnp.sum(hits * gate_probs[:, :, None], axis=1)
    combine_high = combine.astype(bf16)
    combine_low = (combine - combine_high.astype(f32)).astype(bf16)
    both_terms = jnp.concatenate([combine_high, combine_low], axis=0)
    target_half = targets // capacity % 2
    halves = jnp.stack([jnp.where(target_half == i, both_terms, jnp.zeros((), bf16)) for i in range(2)])

    requests, max_blocks = block_table.shape
    head_dim = kv_weight.shape[2]
    flat_weight = kv_weight.reshape(model_width, 2 * head_dim)
    middle = total_slots // 2
    landed = held_until(landed, crossed, order)
    from_y = swapped(landed, "tp", 1)
    from_x = held_until(swapped(landed, "grp", 0), from_y)
    landed_core = swapped(landed, "tp", 0)
    mine = (landed, from_x, from_y)
    theirs = (landed_core, swapped(from_x, "tp", 0), swapped(from_y, "tp", 0))
    by_y = 2 * total_slots // 3
    last_mine = (swapped(from_x[:by_y], "tp", 1), swapped(from_y[by_y:], "grp", 0))

    order = held_until(order, landed_core)
    ordered = crossed.at[order[0]].get(mode="promise_in_bounds")
    arrived = lax.all_to_all(ordered, "grp", split_axis=0, concat_axis=0, tiled=True)

    blocks = jnp.stack(
        [
            (tp_rank ^ (core + 2 * y)) * 2 + (side ^ x)
            for core in range(2)
            for y, x in ((0, 0), (0, 1), (1, 0), (1, 1))
        ]
    ).astype(jnp.int32)
    gate_own, up_own = gate_weight[0].T, up_weight[0].T
    unit_count = gate_own.shape[0]
    sums = call(
        early_units,
        (shape((total_slots, unit_count), f32),) * 2,
        (blocks, *mine, *theirs, gate_own, up_own),
        smem=1,
        name="early_units",
        flops=3 * total_slots * model_width * unit_count,
    )
    last_mine = tuple(held_until(x, *sums) for x in last_mine)
    last_theirs = tuple(swapped(x, "tp", 0) for x in last_mine)
    sums = call(
        late_units,
        (shape((total_slots, eighth), bf16),) * 8,
        (blocks, *last_mine, *last_theirs, *sums, gate_own, up_own, down_weight[0], ordered),
        smem=1,
        away=1,
        name="late_units",
        flops=3 * total_slots * model_width * unit_count,
    )

    draft_count = token_rows // requests
    per_kv = queries.shape[1] // head_dim
    query_rows = queries.reshape(requests, draft_count * per_kv, head_dim)
    pool = jnp.concatenate([decode_cache[:, 0], arrived], axis=0)
    stats = call(
        functools.partial(cached_attention, max_blocks=max_blocks),
        (shape((requests, draft_count * per_kv, head_dim), f32),) * 3,
        (block_table.reshape(-1), lengths, query_rows, pool),
        smem=2,
        name="cached_attention",
        flops=4 * requests * draft_count * per_kv * head_dim * max_blocks * decode_cache.shape[3],
    )

    from_core = tuple(swapped(x, "tp", 0) for x in sums[4:])
    both_ways = (sums[3].astype(f32) + from_core[3].astype(f32)).astype(bf16)
    low, high = swapped(both_ways[:middle], "tp", 1), swapped(both_ways[middle:], "grp", 0)
    to_x, to_y = call(
        turn,
        (shape((total_slots, eighth), bf16),) * 2,
        (sums[1], from_core[1], sums[2], from_core[2], low, high, halves, flat_weight),
        away=2,
        name="turn",
    )
    sum_x, sum_y = swapped(to_x, "grp", 0), swapped(to_y, "tp", 1)
    summed = call(
        join,
        shape((total_slots, eighth), bf16),
        (sums[0], from_core[0], sum_x, sum_y, *stats),
        away=3,
        name="join",
    )
    returned = lax.all_to_all(
        summed.reshape(peer_count, capacity, eighth), "grp", split_axis=0, concat_axis=0, tiled=True
    ).reshape(total_slots, eighth)
    stats = tuple(x.reshape(token_rows, per_kv * head_dim) for x in stats)
    residual_out, scaled = call(
        finish,
        (shape((token_rows, quarter), f32), shape((token_rows, quarter + LANES), bf16)),
        (part, halves, returned, hidden_in, attn_gain.reshape(1, model_width), *stats),
        smem=1,
        away=3,
        name="finish",
    )

    scaled_core = swapped(scaled, "tp", 0)
    scaled_y = swapped(scaled, "tp", 1)
    scaled_diagonal = swapped(scaled_y, "tp", 0)
    fresh_kv, attn_out = call(
        functools.partial(last_step, draft=draft_count),
        (shape((token_rows, 2 * head_dim), bf16), shape((token_rows, per_kv * head_dim), bf16)),
        (part, scaled, scaled_core, scaled_y, scaled_diagonal, flat_weight, queries, *stats),
        smem=1,
        name="last_step",
    )
    return (residual_out, fresh_kv.reshape(token_rows, 2, head_dim), attn_out)


def solution(mesh):
    in_specs = (
        P(("role", "grp"), None),
        P(),
        P(),
        P(("role", "grp"), None),
        P("grp", None, "tp"),
        P("grp", None, "tp"),
        P("grp", "tp", None),
        P(),
        P(None, None, "tp"),
        P(("role", "grp"), "tp"),
        P(("role", "grp"), "tp", None, None, None),
        P(("role", "grp"), "tp", None, None, None),
        P(("role", "grp"), None),
        P(("role", "grp"), None),
        P(("role", "grp")),
    )
    out_specs = (P(("role", "grp"), "tp"), P(("role", "grp"), None, "tp"), P(("role", "grp"), "tp"))
    return jax.shard_map(local, mesh=mesh, in_specs=in_specs, out_specs=out_specs, check_vma=False)
```

```python
import functools

import jax
import jax.numpy as jnp
from jax import lax
from jax.experimental import pallas as pl
from jax.experimental.pallas import tpu as pltpu
from jax.sharding import PartitionSpec as P

epsilon = 1e-06
LANES = 128


def swapped(x, axis, bit):
    return lax.ppermute(x, axis, [(i, i ^ 1 << bit) for i in range(lax.axis_size(axis))])


def inverse_rms(square_sum, width):
    return lax.rsqrt(square_sum / width + epsilon)


def prepare(part_ref, routes_ref, hidden_ref, gain_ref, packed_ref, slots_ref, scale_ref, *, capacity):
    token_rows, model_width = hidden_ref.shape
    peers, _, eighth = packed_ref.shape
    experts = peers // 2
    quarter = 2 * eighth
    f32, bf16 = jnp.float32, jnp.bfloat16
    hidden = hidden_ref[...].astype(f32)
    squares = jnp.sum(hidden * hidden, axis=1, keepdims=True)
    columns = pl.ds(pl.multiple_of(part_ref[0] * quarter, quarter), quarter)
    scale = inverse_rms(squares, model_width)
    scale_ref[...] = jnp.broadcast_to(scale, scale_ref.shape)
    own = hidden_ref[:, columns].astype(f32) * scale * gain_ref[:, columns].astype(f32)
    one_routes, two_routes = routes_ref[0:1, :], routes_ref[1:2, :]
    expert = lax.broadcasted_iota(jnp.int32, (max(experts, 8), token_rows), 0)
    one_hot, two_hot = (expert == one_routes).astype(f32), (expert == two_routes).astype(f32)
    before = lax.broadcasted_iota(jnp.int32, (token_rows, token_rows), 0) < lax.broadcasted_iota(
        jnp.int32, (token_rows, token_rows), 1
    )
    taken = jnp.dot((one_hot + two_hot).astype(bf16), before.astype(f32).astype(bf16), preferred_element_type=f32)
    one_slot = one_routes * capacity + jnp.sum(taken * one_hot, axis=0, keepdims=True).astype(jnp.int32)
    two_slot = two_routes * capacity + jnp.sum(taken * two_hot, axis=0, keepdims=True).astype(jnp.int32)
    slots_ref[0:1, :] = one_slot
    slots_ref[1:2, :] = two_slot
    target = lax.broadcasted_iota(jnp.int32, (experts * capacity, token_rows), 0)
    placing = ((target == one_slot) | (target == two_slot)).astype(f32).astype(bf16)
    packed = jnp.dot(placing, own.astype(bf16), preferred_element_type=f32)
    for e in range(experts):
        for half in range(2):
            block = packed[e * capacity : (e + 1) * capacity, half * eighth : (half + 1) * eighth]
            packed_ref[2 * e + half] = block.astype(bf16)


def wide(a, b):
    return lax.dot_general(a, b, (((1,), (1,)), ((), ())), preferred_element_type=jnp.float32)


def window(blocks_ref, i, size):
    return pl.ds(pl.multiple_of(blocks_ref[i] * size, size), size)


def early_units(blocks_ref, *refs):
    pieces, (gate_ref, up_ref, gate_out, up_out) = refs[:6], refs[6:]
    eighth = pieces[0].shape[1]
    for weight, out in ((gate_ref, gate_out), (up_ref, up_out)):
        total = None
        for i, piece in enumerate(pieces):
            more = wide(piece[...], weight[:, window(blocks_ref, 4 * (i // 3) + i % 3, eighth)])
            total = more if total is None else total + more
        out[...] = total


def late_units(blocks_ref, mine_low, mine_high, theirs_low, theirs_high, gate_sum, up_sum, gate_ref, up_ref, down_ref, *refs):
    outputs = refs[-8:]
    eighth = mine_low.shape[1]
    gate, up = gate_sum[...], up_sum[...]
    for i, low, high in ((3, mine_low, mine_high), (7, theirs_low, theirs_high)):
        piece = jnp.concatenate([low[...], high[...]], axis=0)
        gate = gate + wide(piece, gate_ref[:, window(blocks_ref, i, eighth)])
        up = up + wide(piece, up_ref[:, window(blocks_ref, i, eighth)])
    act = (gate / (1.0 + jnp.exp(-gate)) * up).astype(jnp.bfloat16)
    for i in (3, 7, 2, 6, 1, 5, 0, 4):
        columns = down_ref[:, window(blocks_ref, i, eighth)]
        outputs[i][...] = jnp.dot(act, columns, preferred_element_type=jnp.float32).astype(jnp.bfloat16)


def turn(mine_x, theirs_x, mine_y, theirs_y, low_ref, high_ref, *refs):
    x_ref, y_ref = refs[-2:]
    split = low_ref.shape[0]
    low, high = slice(0, split), slice(split, x_ref.shape[0])
    for mine, theirs, far, extra, plain, out in (
        (mine_x, theirs_x, low_ref, low, high, x_ref),
        (mine_y, theirs_y, high_ref, high, low, y_ref),
    ):
        out[plain] = (mine[plain].astype(jnp.float32) + theirs[plain].astype(jnp.float32)).astype(jnp.bfloat16)
        total = mine[extra].astype(jnp.float32) + theirs[extra].astype(jnp.float32) + far[...].astype(jnp.float32)
        out[extra] = total.astype(jnp.bfloat16)


def join(mine_ref, theirs_ref, x_ref, y_ref, *refs):
    total = mine_ref[...].astype(jnp.float32) + theirs_ref[...].astype(jnp.float32)
    total = total + x_ref[...].astype(jnp.float32) + y_ref[...].astype(jnp.float32)
    refs[-1][...] = total.astype(jnp.bfloat16)


def held_until(x, *others):
    def kernel(*refs):
        pass

    any_space = pl.BlockSpec(memory_space=pl.ANY)
    return pl.pallas_call(
        kernel,
        out_shape=jax.ShapeDtypeStruct(x.shape, x.dtype),
        in_specs=[any_space] * (1 + len(others)),
        out_specs=any_space,
        input_output_aliases={0: 0},
        name="held_until",
    )(x, *others)


def finish(part_ref, combine_ref, returned_ref, hidden_ref, gain_ref, *refs):
    f32, bf16 = jnp.float32, jnp.bfloat16
    residual_ref, scaled_ref = refs[-2:]
    token_rows = hidden_ref.shape[0]
    eighth = returned_ref.shape[1]
    quarter = 2 * eighth
    squares = jnp.zeros((token_rows, 1), f32)
    for half in range(2):
        start = pl.multiple_of(part_ref[0] * quarter + half * eighth, eighth)
        terms = jnp.dot(combine_ref[half], returned_ref[...], preferred_element_type=f32)
        moe = terms[:token_rows] + terms[token_rows:]
        value = hidden_ref[:, pl.ds(start, eighth)].astype(f32) + moe
        residual_ref[:, half * eighth : (half + 1) * eighth] = value
        scaled_ref[:, half * eighth : (half + 1) * eighth] = (value * gain_ref[:, pl.ds(start, eighth)].astype(f32)).astype(bf16)
        squares = squares + jnp.sum(value * value, axis=1, keepdims=True)
    high = squares.astype(bf16).astype(f32)
    lane = lax.broadcasted_iota(jnp.int32, (token_rows, LANES), 1)
    extra = jnp.where(lane == 0, high, jnp.where(lane == 1, squares - high, 0.0))
    scaled_ref[:, quarter:] = extra.astype(bf16)


def last_step(part_ref, own_ref, core_ref, y_ref, diagonal_ref, weight_ref, query_ref, top_ref, total_ref, mixed_ref, kv_ref, out_ref, *, draft):
    f32, bf16 = jnp.float32, jnp.bfloat16
    token_rows = query_ref.shape[0]
    head_dim = kv_ref.shape[1] // 2
    quarter = own_ref.shape[1] - LANES
    parts = (own_ref, core_ref, y_ref, diagonal_ref)
    squares = jnp.zeros((token_rows, LANES), f32)
    fresh = jnp.zeros((token_rows, 2 * head_dim), f32)
    for i, ref in enumerate(parts):
        rows = pl.ds(pl.multiple_of((part_ref[0] ^ i) * quarter, quarter), quarter)
        fresh = fresh + jnp.dot(ref[:, :quarter], weight_ref[rows, :], preferred_element_type=f32)
        squares = squares + ref[:, quarter:].astype(f32)
    square_sum = jnp.sum(squares, axis=1, keepdims=True)
    fresh = (fresh * inverse_rms(square_sum, len(parts) * quarter)).astype(bf16)
    kv_ref[...] = fresh
    keys = fresh[:, :head_dim]
    values = jnp.concatenate([fresh[:, head_dim:], jnp.ones((token_rows, head_dim), bf16)], axis=1)
    row = lax.broadcasted_iota(jnp.int32, (token_rows, token_rows), 0)
    col = lax.broadcasted_iota(jnp.int32, (token_rows, token_rows), 1)
    seen = (row // draft == col // draft) & (col <= row)
    for h in range(query_ref.shape[1] // head_dim):
        lanes = slice(h * head_dim, (h + 1) * head_dim)
        scores = jnp.where(seen, wide(query_ref[:, lanes], keys) * head_dim ** (-0.5), -jnp.inf)
        top = top_ref[:, lanes]
        new_top = jnp.maximum(top, jnp.max(scores, axis=1, keepdims=True))
        shrink = jnp.exp(top - new_top)
        recent = jnp.dot(jnp.exp(scores - new_top).astype(bf16), values, preferred_element_type=f32)
        denom = shrink * total_ref[:, lanes] + recent[:, head_dim:]
        out_ref[:, lanes] = ((mixed_ref[:, lanes] * shrink + recent[:, :head_dim]) / denom).astype(bf16)


def call(kernel, out_shape, args, smem=0, name=None, away=0, flops=0):
    spaces = [pltpu.SMEM] * smem + [pltpu.VMEM] * (len(args) - smem - away) + [pl.ANY] * away
    out_specs = jax.tree.map(lambda _: pl.BlockSpec(memory_space=pltpu.VMEM), out_shape)
    moved = sum(x.size * x.dtype.itemsize for x in list(args) + jax.tree.leaves(out_shape))
    return pl.pallas_call(
        kernel,
        out_shape=out_shape,
        in_specs=[pl.BlockSpec(memory_space=space) for space in spaces],
        out_specs=out_specs,
        compiler_params=pltpu.CompilerParams(vmem_limit_bytes=48 << 20),
        cost_estimate=pl.CostEstimate(flops=flops, transcendentals=0, bytes_accessed=moved),
        name=name,
    )(*args)


def cached_attention(table_ref, length_ref, query_ref, pool_ref, top_ref, total_ref, mixed_ref, *, max_blocks):
    requests, rows, head_dim = query_ref.shape
    block_len = pool_ref.shape[2]
    span = max_blocks * block_len
    scale = head_dim ** (-0.5)
    places = lax.broadcasted_iota(jnp.int32, (rows, span), 1)
    ones = jnp.ones((span, head_dim), jnp.bfloat16)

    def one(r, carry):
        ids = [table_ref[r * max_blocks + b] for b in range(max_blocks)]
        keys = jnp.concatenate([pool_ref[i, 0] for i in ids], axis=0)
        values = jnp.concatenate([pool_ref[i, 1] for i in ids], axis=0)
        values = jnp.concatenate([values, ones], axis=1)
        scores = lax.dot_general(
            query_ref[r], keys, (((1,), (1,)), ((), ())), preferred_element_type=jnp.float32
        )
        scores = jnp.where(places < length_ref[r], scores * scale, -jnp.inf)
        top = jnp.max(scores, axis=1, keepdims=True)
        exps = jnp.exp(scores - top)
        mixed = jnp.dot(exps.astype(jnp.bfloat16), values, preferred_element_type=jnp.float32)
        top_ref[r] = jnp.broadcast_to(top, (rows, head_dim))
        total_ref[r] = mixed[:, head_dim:]
        mixed_ref[r] = mixed[:, :head_dim]
        return carry

    lax.fori_loop(0, requests, one, 0, unroll=2)


def local(
    hidden_in,
    moe_gain,
    router,
    routes,
    gate_weight,
    up_weight,
    down_weight,
    attn_gain,
    kv_weight,
    queries,
    decode_cache,
    prompt_cache,
    handoff,
    block_table,
    lengths,
):
    peer_count = lax.axis_size("grp")
    expert_count = peer_count // 2
    tp_count = lax.axis_size("tp")
    tp_rank = lax.axis_index("tp")
    token_rows, model_width = hidden_in.shape
    picks_per = routes.shape[1]
    quarter = model_width // tp_count
    capacity = min(token_rows, 3 * token_rows * picks_per // (2 * expert_count))
    total_slots = 2 * expert_count * capacity
    eighth = quarter // 2
    f32, bf16 = jnp.float32, jnp.bfloat16
    shape = jax.ShapeDtypeStruct
    side = lax.axis_index("grp") & 1
    part = tp_rank.astype(jnp.int32).reshape(1)

    packed, slots, scale_in = call(
        functools.partial(prepare, capacity=capacity),
        (shape((peer_count, capacity, eighth), bf16), shape((picks_per, token_rows), jnp.int32), shape((token_rows, LANES), f32)),
        (part, routes.T, hidden_in, moe_gain.reshape(1, model_width)),
        smem=1,
        name="prepare",
    )
    landed = lax.all_to_all(packed, "grp", split_axis=0, concat_axis=0, tiled=True)
    landed = landed.reshape(total_slots, eighth)

    crossed = swapped(prompt_cache[:, 0], "role", 0)
    order = swapped(handoff, "role", 0)

    hidden = hidden_in.astype(f32)
    moe_in = (hidden * scale_in[:, :1] * moe_gain.astype(f32)).astype(bf16)
    logits = jnp.dot(moe_in, router, preferred_element_type=f32)
    gate_probs = jax.nn.softmax(jnp.take_along_axis(logits, routes, axis=1), axis=1)
    targets = jnp.arange(total_slots, dtype=jnp.int32)
    target_slot = targets // (2 * capacity) * capacity + targets % capacity
    hits = (slots.T[:, :, None] == target_slot).astype(f32)
    combine = jnp.sum(hits * gate_probs[:, :, None], axis=1)
    combine_high = combine.astype(bf16)
    combine_low = (combine - combine_high.astype(f32)).astype(bf16)
    both_terms = jnp.concatenate([combine_high, combine_low], axis=0)
    target_half = targets // capacity % 2
    halves = jnp.stack([jnp.where(target_half == i, both_terms, jnp.zeros((), bf16)) for i in range(2)])

    requests, max_blocks = block_table.shape
    head_dim = kv_weight.shape[2]
    flat_weight = kv_weight.reshape(model_width, 2 * head_dim)
    landed = held_until(landed, crossed, order)
    from_y = swapped(landed, "tp", 1)
    landed_core = swapped(landed, "tp", 0)
    ordered = crossed.at[held_until(order, landed_core)[0]].get(mode="promise_in_bounds")
    from_x = held_until(swapped(landed, "grp", 0), from_y, ordered)
    mine = (landed, from_x, from_y)
    theirs = (landed_core, swapped(from_x, "tp", 0), swapped(from_y, "tp", 0))
    by_y = 2 * total_slots // 3
    last_mine = (swapped(from_x[:by_y], "tp", 1), swapped(from_y[by_y:], "grp", 0))

    blocks = jnp.stack(
        [
            (tp_rank ^ (core + 2 * y)) * 2 + (side ^ x)
            for core in range(2)
            for y, x in ((0, 0), (0, 1), (1, 0), (1, 1))
        ]
    ).astype(jnp.int32)
    gate_own, up_own = gate_weight[0].T, up_weight[0].T
    unit_count = gate_own.shape[0]
    sums = call(
        early_units,
        (shape((total_slots, unit_count), f32),) * 2,
        (blocks, *mine, *theirs, gate_own, up_own),
        smem=1,
        name="early_units",
        flops=3 * total_slots * model_width * unit_count,
    )
    ordered = held_until(ordered, *sums)
    arrived = lax.all_to_all(ordered, "grp", split_axis=0, concat_axis=0, tiled=True)
    last_mine = tuple(held_until(x, *sums) for x in last_mine)
    last_theirs = tuple(swapped(x, "tp", 0) for x in last_mine)
    sums = call(
        late_units,
        (shape((total_slots, eighth), bf16),) * 8,
        (blocks, *last_mine, *last_theirs, *sums, gate_own, up_own, down_weight[0], ordered),
        smem=1,
        away=1,
        name="late_units",
        flops=3 * total_slots * model_width * unit_count,
    )

    draft_count = token_rows // requests
    per_kv = queries.shape[1] // head_dim
    query_rows = queries.reshape(requests, draft_count * per_kv, head_dim)
    pool = jnp.concatenate([decode_cache[:, 0], arrived], axis=0)
    stats = call(
        functools.partial(cached_attention, max_blocks=max_blocks),
        (shape((requests, draft_count * per_kv, head_dim), f32),) * 3,
        (block_table.reshape(-1), lengths, query_rows, pool),
        smem=2,
        name="cached_attention",
        flops=4 * requests * draft_count * per_kv * head_dim * max_blocks * decode_cache.shape[3],
    )

    from_core = tuple(swapped(x, "tp", 0) for x in sums[4:])
    both_ways = (sums[3].astype(f32) + from_core[3].astype(f32)).astype(bf16)
    low, high = swapped(both_ways[:by_y], "tp", 1), swapped(both_ways[by_y:], "grp", 0)
    to_x, to_y = call(
        turn,
        (shape((total_slots, eighth), bf16),) * 2,
        (sums[1], from_core[1], sums[2], from_core[2], low, high, halves, flat_weight),
        away=2,
        name="turn",
    )
    sum_x, sum_y = swapped(to_x, "grp", 0), swapped(to_y, "tp", 1)
    summed = call(
        join,
        shape((total_slots, eighth), bf16),
        (sums[0], from_core[0], sum_x, sum_y, *stats),
        away=3,
        name="join",
    )
    returned = lax.all_to_all(
        summed.reshape(peer_count, capacity, eighth), "grp", split_axis=0, concat_axis=0, tiled=True
    ).reshape(total_slots, eighth)
    stats = tuple(x.reshape(token_rows, per_kv * head_dim) for x in stats)
    residual_out, scaled = call(
        finish,
        (shape((token_rows, quarter), f32), shape((token_rows, quarter + LANES), bf16)),
        (part, halves, returned, hidden_in, attn_gain.reshape(1, model_width), *stats),
        smem=1,
        away=3,
        name="finish",
    )

    scaled_core = swapped(scaled, "tp", 0)
    scaled_y = swapped(scaled, "tp", 1)
    scaled_diagonal = swapped(scaled_y, "tp", 0)
    fresh_kv, attn_out = call(
        functools.partial(last_step, draft=draft_count),
        (shape((token_rows, 2 * head_dim), bf16), shape((token_rows, per_kv * head_dim), bf16)),
        (part, scaled, scaled_core, scaled_y, scaled_diagonal, flat_weight, queries, *stats),
        smem=1,
        name="last_step",
    )
    return (residual_out, fresh_kv.reshape(token_rows, 2, head_dim), attn_out)


def solution(mesh):
    in_specs = (
        P(("role", "grp"), None),
        P(),
        P(),
        P(("role", "grp"), None),
        P("grp", None, "tp"),
        P("grp", None, "tp"),
        P("grp", "tp", None),
        P(),
        P(None, None, "tp"),
        P(("role", "grp"), "tp"),
        P(("role", "grp"), "tp", None, None, None),
        P(("role", "grp"), "tp", None, None, None),
        P(("role", "grp"), None),
        P(("role", "grp"), None),
        P(("role", "grp")),
    )
    out_specs = (P(("role", "grp"), "tp"), P(("role", "grp"), None, "tp"), P(("role", "grp"), "tp"))
    return jax.shard_map(local, mesh=mesh, in_specs=in_specs, out_specs=out_specs, check_vma=False)
```

```python
import functools

import jax
import jax.numpy as jnp
from jax import lax
from jax.experimental import pallas as pl
from jax.experimental.pallas import tpu as pltpu
from jax.sharding import PartitionSpec as P

epsilon = 1e-06
LANES = 128


def swapped(x, axis, bit):
    return lax.ppermute(x, axis, [(i, i ^ 1 << bit) for i in range(lax.axis_size(axis))])


def inverse_rms(square_sum, width):
    return lax.rsqrt(square_sum / width + epsilon)


def prepare(part_ref, routes_ref, hidden_ref, gain_ref, packed_ref, slots_ref, scale_ref, *, capacity):
    token_rows, model_width = hidden_ref.shape
    peers, _, eighth = packed_ref.shape
    experts = peers // 2
    quarter = 2 * eighth
    f32, bf16 = jnp.float32, jnp.bfloat16
    hidden = hidden_ref[...].astype(f32)
    squares = jnp.sum(hidden * hidden, axis=1, keepdims=True)
    columns = pl.ds(pl.multiple_of(part_ref[0] * quarter, quarter), quarter)
    scale = inverse_rms(squares, model_width)
    scale_ref[...] = jnp.broadcast_to(scale, scale_ref.shape)
    own = hidden_ref[:, columns].astype(f32) * scale * gain_ref[:, columns].astype(f32)
    one_routes, two_routes = routes_ref[0:1, :], routes_ref[1:2, :]
    expert = lax.broadcasted_iota(jnp.int32, (max(experts, 8), token_rows), 0)
    one_hot, two_hot = (expert == one_routes).astype(f32), (expert == two_routes).astype(f32)
    before = lax.broadcasted_iota(jnp.int32, (token_rows, token_rows), 0) < lax.broadcasted_iota(
        jnp.int32, (token_rows, token_rows), 1
    )
    taken = jnp.dot((one_hot + two_hot).astype(bf16), before.astype(f32).astype(bf16), preferred_element_type=f32)
    one_slot = one_routes * capacity + jnp.sum(taken * one_hot, axis=0, keepdims=True).astype(jnp.int32)
    two_slot = two_routes * capacity + jnp.sum(taken * two_hot, axis=0, keepdims=True).astype(jnp.int32)
    slots_ref[0:1, :] = one_slot
    slots_ref[1:2, :] = two_slot
    target = lax.broadcasted_iota(jnp.int32, (experts * capacity, token_rows), 0)
    placing = ((target == one_slot) | (target == two_slot)).astype(f32).astype(bf16)
    packed = jnp.dot(placing, own.astype(bf16), preferred_element_type=f32)
    for e in range(experts):
        for half in range(2):
            block = packed[e * capacity : (e + 1) * capacity, half * eighth : (half + 1) * eighth]
            packed_ref[2 * e + half] = block.astype(bf16)


def wide(a, b):
    return lax.dot_general(a, b, (((1,), (1,)), ((), ())), preferred_element_type=jnp.float32)


def window(blocks_ref, i, size):
    return pl.ds(pl.multiple_of(blocks_ref[i] * size, size), size)


def early_units(blocks_ref, *refs):
    pieces, (gate_ref, up_ref, gate_out, up_out) = refs[:6], refs[6:]
    eighth = pieces[0].shape[1]
    for weight, out in ((gate_ref, gate_out), (up_ref, up_out)):
        total = None
        for i, piece in enumerate(pieces):
            more = wide(piece[...], weight[:, window(blocks_ref, 4 * (i // 3) + i % 3, eighth)])
            total = more if total is None else total + more
        out[...] = total


def late_units(blocks_ref, mine_low, mine_high, theirs_low, theirs_high, gate_sum, up_sum, gate_ref, up_ref, down_ref, *refs):
    outputs = refs[-8:]
    eighth = mine_low.shape[1]
    gate, up = gate_sum[...], up_sum[...]
    for i, low, high in ((3, mine_low, mine_high), (7, theirs_low, theirs_high)):
        piece = jnp.concatenate([low[...], high[...]], axis=0)
        gate = gate + wide(piece, gate_ref[:, window(blocks_ref, i, eighth)])
        up = up + wide(piece, up_ref[:, window(blocks_ref, i, eighth)])
    act = (gate / (1.0 + jnp.exp(-gate)) * up).astype(jnp.bfloat16)
    for i in (3, 7, 2, 6, 1, 5, 0, 4):
        columns = down_ref[:, window(blocks_ref, i, eighth)]
        outputs[i][...] = jnp.dot(act, columns, preferred_element_type=jnp.float32).astype(jnp.bfloat16)


def turn(mine_x, theirs_x, mine_y, theirs_y, low_ref, high_ref, *refs):
    x_ref, y_ref = refs[-2:]
    split = low_ref.shape[0]
    low, high = slice(0, split), slice(split, x_ref.shape[0])
    for mine, theirs, far, extra, plain, out in (
        (mine_x, theirs_x, low_ref, low, high, x_ref),
        (mine_y, theirs_y, high_ref, high, low, y_ref),
    ):
        out[plain] = (mine[plain].astype(jnp.float32) + theirs[plain].astype(jnp.float32)).astype(jnp.bfloat16)
        total = mine[extra].astype(jnp.float32) + theirs[extra].astype(jnp.float32) + far[...].astype(jnp.float32)
        out[extra] = total.astype(jnp.bfloat16)


def join(mine_ref, theirs_ref, x_ref, y_ref, *refs):
    total = mine_ref[...].astype(jnp.float32) + theirs_ref[...].astype(jnp.float32)
    total = total + x_ref[...].astype(jnp.float32) + y_ref[...].astype(jnp.float32)
    refs[-1][...] = total.astype(jnp.bfloat16)


def held_until(x, *others):
    def kernel(*refs):
        pass

    any_space = pl.BlockSpec(memory_space=pl.ANY)
    return pl.pallas_call(
        kernel,
        out_shape=jax.ShapeDtypeStruct(x.shape, x.dtype),
        in_specs=[any_space] * (1 + len(others)),
        out_specs=any_space,
        input_output_aliases={0: 0},
        name="held_until",
    )(x, *others)


def finish(part_ref, combine_ref, returned_ref, hidden_ref, gain_ref, *refs):
    f32, bf16 = jnp.float32, jnp.bfloat16
    residual_ref, scaled_ref = refs[-2:]
    token_rows = hidden_ref.shape[0]
    eighth = returned_ref.shape[1]
    quarter = 2 * eighth
    squares = jnp.zeros((token_rows, 1), f32)
    for half in range(2):
        start = pl.multiple_of(part_ref[0] * quarter + half * eighth, eighth)
        terms = jnp.dot(combine_ref[half], returned_ref[...], preferred_element_type=f32)
        moe = terms[:token_rows] + terms[token_rows:]
        value = hidden_ref[:, pl.ds(start, eighth)].astype(f32) + moe
        residual_ref[:, half * eighth : (half + 1) * eighth] = value
        scaled_ref[:, half * eighth : (half + 1) * eighth] = (value * gain_ref[:, pl.ds(start, eighth)].astype(f32)).astype(bf16)
        squares = squares + jnp.sum(value * value, axis=1, keepdims=True)
    high = squares.astype(bf16).astype(f32)
    lane = lax.broadcasted_iota(jnp.int32, (token_rows, LANES), 1)
    extra = jnp.where(lane == 0, high, jnp.where(lane == 1, squares - high, 0.0))
    scaled_ref[:, quarter:] = extra.astype(bf16)


def last_step(part_ref, own_ref, core_ref, y_ref, diagonal_ref, weight_ref, query_ref, top_ref, total_ref, mixed_ref, kv_ref, out_ref, *, draft):
    f32, bf16 = jnp.float32, jnp.bfloat16
    token_rows = query_ref.shape[0]
    head_dim = kv_ref.shape[1] // 2
    quarter = own_ref.shape[1] - LANES
    parts = (own_ref, core_ref, y_ref, diagonal_ref)
    squares = jnp.zeros((token_rows, LANES), f32)
    fresh = jnp.zeros((token_rows, 2 * head_dim), f32)
    for i, ref in enumerate(parts):
        rows = pl.ds(pl.multiple_of((part_ref[0] ^ i) * quarter, quarter), quarter)
        fresh = fresh + jnp.dot(ref[:, :quarter], weight_ref[rows, :], preferred_element_type=f32)
        squares = squares + ref[:, quarter:].astype(f32)
    square_sum = jnp.sum(squares, axis=1, keepdims=True)
    fresh = (fresh * inverse_rms(square_sum, len(parts) * quarter)).astype(bf16)
    kv_ref[...] = fresh
    keys = fresh[:, :head_dim]
    values = jnp.concatenate([fresh[:, head_dim:], jnp.ones((token_rows, head_dim), bf16)], axis=1)
    row = lax.broadcasted_iota(jnp.int32, (token_rows, token_rows), 0)
    col = lax.broadcasted_iota(jnp.int32, (token_rows, token_rows), 1)
    seen = (row // draft == col // draft) & (col <= row)
    for h in range(query_ref.shape[1] // head_dim):
        lanes = slice(h * head_dim, (h + 1) * head_dim)
        scores = jnp.where(seen, wide(query_ref[:, lanes], keys) * head_dim ** (-0.5), -jnp.inf)
        top = top_ref[:, lanes]
        new_top = jnp.maximum(top, jnp.max(scores, axis=1, keepdims=True))
        shrink = jnp.exp(top - new_top)
        recent = jnp.dot(jnp.exp(scores - new_top).astype(bf16), values, preferred_element_type=f32)
        denom = shrink * total_ref[:, lanes] + recent[:, head_dim:]
        out_ref[:, lanes] = ((mixed_ref[:, lanes] * shrink + recent[:, :head_dim]) / denom).astype(bf16)


def call(kernel, out_shape, args, smem=0, name=None, away=0, flops=0):
    spaces = [pltpu.SMEM] * smem + [pltpu.VMEM] * (len(args) - smem - away) + [pl.ANY] * away
    out_specs = jax.tree.map(lambda _: pl.BlockSpec(memory_space=pltpu.VMEM), out_shape)
    moved = sum(x.size * x.dtype.itemsize for x in list(args) + jax.tree.leaves(out_shape))
    return pl.pallas_call(
        kernel,
        out_shape=out_shape,
        in_specs=[pl.BlockSpec(memory_space=space) for space in spaces],
        out_specs=out_specs,
        compiler_params=pltpu.CompilerParams(vmem_limit_bytes=48 << 20),
        cost_estimate=pl.CostEstimate(flops=flops, transcendentals=0, bytes_accessed=moved),
        name=name,
    )(*args)


def cached_attention(table_ref, length_ref, query_ref, pool_ref, top_ref, total_ref, mixed_ref, *, max_blocks):
    requests, rows, head_dim = query_ref.shape
    block_len = pool_ref.shape[2]
    span = max_blocks * block_len
    scale = head_dim ** (-0.5)
    places = lax.broadcasted_iota(jnp.int32, (rows, span), 1)
    ones = jnp.ones((span, head_dim), jnp.bfloat16)

    def one(r, carry):
        ids = [table_ref[r * max_blocks + b] for b in range(max_blocks)]
        keys = jnp.concatenate([pool_ref[i, 0] for i in ids], axis=0)
        values = jnp.concatenate([pool_ref[i, 1] for i in ids], axis=0)
        values = jnp.concatenate([values, ones], axis=1)
        scores = lax.dot_general(
            query_ref[r], keys, (((1,), (1,)), ((), ())), preferred_element_type=jnp.float32
        )
        scores = jnp.where(places < length_ref[r], scores * scale, -jnp.inf)
        top = jnp.max(scores, axis=1, keepdims=True)
        exps = jnp.exp(scores - top)
        mixed = jnp.dot(exps.astype(jnp.bfloat16), values, preferred_element_type=jnp.float32)
        top_ref[r] = jnp.broadcast_to(top, (rows, head_dim))
        total_ref[r] = mixed[:, head_dim:]
        mixed_ref[r] = mixed[:, :head_dim]
        return carry

    lax.fori_loop(0, requests, one, 0, unroll=2)


def local(
    hidden_in,
    moe_gain,
    router,
    routes,
    gate_weight,
    up_weight,
    down_weight,
    attn_gain,
    kv_weight,
    queries,
    decode_cache,
    prompt_cache,
    handoff,
    block_table,
    lengths,
):
    peer_count = lax.axis_size("grp")
    expert_count = peer_count // 2
    tp_count = lax.axis_size("tp")
    tp_rank = lax.axis_index("tp")
    token_rows, model_width = hidden_in.shape
    picks_per = routes.shape[1]
    quarter = model_width // tp_count
    capacity = min(token_rows, 3 * token_rows * picks_per // (2 * expert_count))
    total_slots = 2 * expert_count * capacity
    eighth = quarter // 2
    f32, bf16 = jnp.float32, jnp.bfloat16
    shape = jax.ShapeDtypeStruct
    side = lax.axis_index("grp") & 1
    part = tp_rank.astype(jnp.int32).reshape(1)

    packed, slots, scale_in = call(
        functools.partial(prepare, capacity=capacity),
        (shape((peer_count, capacity, eighth), bf16), shape((picks_per, token_rows), jnp.int32), shape((token_rows, LANES), f32)),
        (part, routes.T, hidden_in, moe_gain.reshape(1, model_width)),
        smem=1,
        name="prepare",
    )
    landed = lax.all_to_all(packed, "grp", split_axis=0, concat_axis=0, tiled=True)
    landed = landed.reshape(total_slots, eighth)

    crossed = swapped(prompt_cache[:, 0], "role", 0)
    order = swapped(handoff, "role", 0)

    hidden = hidden_in.astype(f32)
    moe_in = (hidden * scale_in[:, :1] * moe_gain.astype(f32)).astype(bf16)
    logits = jnp.dot(moe_in, router, preferred_element_type=f32)
    gate_probs = jax.nn.softmax(jnp.take_along_axis(logits, routes, axis=1), axis=1)
    targets = jnp.arange(total_slots, dtype=jnp.int32)
    target_slot = targets // (2 * capacity) * capacity + targets % capacity
    hits = (slots.T[:, :, None] == target_slot).astype(f32)
    combine = jnp.sum(hits * gate_probs[:, :, None], axis=1)
    combine_high = combine.astype(bf16)
    combine_low = (combine - combine_high.astype(f32)).astype(bf16)
    both_terms = jnp.concatenate([combine_high, combine_low], axis=0)
    target_half = targets // capacity % 2
    halves = jnp.stack([jnp.where(target_half == i, both_terms, jnp.zeros((), bf16)) for i in range(2)])

    requests, max_blocks = block_table.shape
    head_dim = kv_weight.shape[2]
    flat_weight = kv_weight.reshape(model_width, 2 * head_dim)
    landed = held_until(landed, crossed, order)
    from_y = swapped(landed, "tp", 1)
    landed_core = swapped(landed, "tp", 0)
    ordered = crossed.at[held_until(order, landed_core)[0]].get(mode="promise_in_bounds")
    from_x = held_until(swapped(landed, "grp", 0), from_y, ordered)
    mine = (landed, from_x, from_y)
    theirs = (landed_core, swapped(from_x, "tp", 0), swapped(from_y, "tp", 0))
    by_y = 2 * total_slots // 3
    last_mine = (swapped(from_x[:by_y], "tp", 1), swapped(from_y[by_y:], "grp", 0))

    blocks = jnp.stack(
        [
            (tp_rank ^ (core + 2 * y)) * 2 + (side ^ x)
            for core in range(2)
            for y, x in ((0, 0), (0, 1), (1, 0), (1, 1))
        ]
    ).astype(jnp.int32)
    gate_own, up_own = gate_weight[0].T, up_weight[0].T
    unit_count = gate_own.shape[0]
    sums = call(
        early_units,
        (shape((total_slots, unit_count), f32),) * 2,
        (blocks, *mine, *theirs, gate_own, up_own),
        smem=1,
        name="early_units",
        flops=3 * total_slots * model_width * unit_count,
    )
    arrived = lax.all_to_all(ordered, "grp", split_axis=0, concat_axis=0, tiled=True)
    last_mine = tuple(held_until(x, *sums) for x in last_mine)
    last_theirs = tuple(swapped(x, "tp", 0) for x in last_mine)
    sums = call(
        late_units,
        (shape((total_slots, eighth), bf16),) * 8,
        (blocks, *last_mine, *last_theirs, *sums, gate_own, up_own, down_weight[0]),
        smem=1,
        name="late_units",
        flops=3 * total_slots * model_width * unit_count,
    )

    draft_count = token_rows // requests
    per_kv = queries.shape[1] // head_dim
    query_rows = queries.reshape(requests, draft_count * per_kv, head_dim)
    pool = jnp.concatenate([decode_cache[:, 0], arrived], axis=0)
    stats = call(
        functools.partial(cached_attention, max_blocks=max_blocks),
        (shape((requests, draft_count * per_kv, head_dim), f32),) * 3,
        (block_table.reshape(-1), lengths, query_rows, pool),
        smem=2,
        name="cached_attention",
        flops=4 * requests * draft_count * per_kv * head_dim * max_blocks * decode_cache.shape[3],
    )

    from_core = tuple(swapped(x, "tp", 0) for x in sums[4:])
    both_ways = (sums[3].astype(f32) + from_core[3].astype(f32)).astype(bf16)
    both_ways = held_until(both_ways, arrived)
    low, high = swapped(both_ways[:by_y], "tp", 1), swapped(both_ways[by_y:], "grp", 0)
    to_x, to_y = call(
        turn,
        (shape((total_slots, eighth), bf16),) * 2,
        (sums[1], from_core[1], sums[2], from_core[2], low, high, halves, flat_weight),
        away=2,
        name="turn",
    )
    sum_x, sum_y = swapped(to_x, "grp", 0), swapped(to_y, "tp", 1)
    summed = call(
        join,
        shape((total_slots, eighth), bf16),
        (sums[0], from_core[0], sum_x, sum_y, *stats),
        away=3,
        name="join",
    )
    returned = lax.all_to_all(
        summed.reshape(peer_count, capacity, eighth), "grp", split_axis=0, concat_axis=0, tiled=True
    ).reshape(total_slots, eighth)
    stats = tuple(x.reshape(token_rows, per_kv * head_dim) for x in stats)
    residual_out, scaled = call(
        finish,
        (shape((token_rows, quarter), f32), shape((token_rows, quarter + LANES), bf16)),
        (part, halves, returned, hidden_in, attn_gain.reshape(1, model_width), *stats),
        smem=1,
        away=3,
        name="finish",
    )

    scaled_core = swapped(scaled, "tp", 0)
    scaled_y = swapped(scaled, "tp", 1)
    scaled_diagonal = swapped(scaled_y, "tp", 0)
    fresh_kv, attn_out = call(
        functools.partial(last_step, draft=draft_count),
        (shape((token_rows, 2 * head_dim), bf16), shape((token_rows, per_kv * head_dim), bf16)),
        (part, scaled, scaled_core, scaled_y, scaled_diagonal, flat_weight, queries, *stats),
        smem=1,
        name="last_step",
    )
    return (residual_out, fresh_kv.reshape(token_rows, 2, head_dim), attn_out)


def solution(mesh):
    in_specs = (
        P(("role", "grp"), None),
        P(),
        P(),
        P(("role", "grp"), None),
        P("grp", None, "tp"),
        P("grp", None, "tp"),
        P("grp", "tp", None),
        P(),
        P(None, None, "tp"),
        P(("role", "grp"), "tp"),
        P(("role", "grp"), "tp", None, None, None),
        P(("role", "grp"), "tp", None, None, None),
        P(("role", "grp"), None),
        P(("role", "grp"), None),
        P(("role", "grp")),
    )
    out_specs = (P(("role", "grp"), "tp"), P(("role", "grp"), None, "tp"), P(("role", "grp"), "tp"))
    return jax.shard_map(local, mesh=mesh, in_specs=in_specs, out_specs=out_specs, check_vma=False)
```

```python
import functools

import jax
import jax.numpy as jnp
from jax import lax
from jax.experimental import pallas as pl
from jax.experimental.pallas import tpu as pltpu
from jax.sharding import PartitionSpec as P

epsilon = 1e-06
LANES = 128


def swapped(x, axis, bit):
    return lax.ppermute(x, axis, [(i, i ^ 1 << bit) for i in range(lax.axis_size(axis))])


def inverse_rms(square_sum, width):
    return lax.rsqrt(square_sum / width + epsilon)


def prepare(part_ref, routes_ref, hidden_ref, gain_ref, packed_ref, slots_ref, scale_ref, *, capacity):
    token_rows, model_width = hidden_ref.shape
    peers, _, eighth = packed_ref.shape
    experts = peers // 2
    quarter = 2 * eighth
    f32, bf16 = jnp.float32, jnp.bfloat16
    hidden = hidden_ref[...].astype(f32)
    squares = jnp.sum(hidden * hidden, axis=1, keepdims=True)
    columns = pl.ds(pl.multiple_of(part_ref[0] * quarter, quarter), quarter)
    scale = inverse_rms(squares, model_width)
    scale_ref[...] = jnp.broadcast_to(scale, scale_ref.shape)
    own = hidden_ref[:, columns].astype(f32) * scale * gain_ref[:, columns].astype(f32)
    one_routes, two_routes = routes_ref[0:1, :], routes_ref[1:2, :]
    expert = lax.broadcasted_iota(jnp.int32, (max(experts, 8), token_rows), 0)
    one_hot, two_hot = (expert == one_routes).astype(f32), (expert == two_routes).astype(f32)
    before = lax.broadcasted_iota(jnp.int32, (token_rows, token_rows), 0) < lax.broadcasted_iota(
        jnp.int32, (token_rows, token_rows), 1
    )
    taken = jnp.dot((one_hot + two_hot).astype(bf16), before.astype(f32).astype(bf16), preferred_element_type=f32)
    one_slot = one_routes * capacity + jnp.sum(taken * one_hot, axis=0, keepdims=True).astype(jnp.int32)
    two_slot = two_routes * capacity + jnp.sum(taken * two_hot, axis=0, keepdims=True).astype(jnp.int32)
    slots_ref[0:1, :] = one_slot
    slots_ref[1:2, :] = two_slot
    target = lax.broadcasted_iota(jnp.int32, (experts * capacity, token_rows), 0)
    placing = ((target == one_slot) | (target == two_slot)).astype(f32).astype(bf16)
    packed = jnp.dot(placing, own.astype(bf16), preferred_element_type=f32)
    for e in range(experts):
        for half in range(2):
            block = packed[e * capacity : (e + 1) * capacity, half * eighth : (half + 1) * eighth]
            packed_ref[2 * e + half] = block.astype(bf16)


def wide(a, b):
    return lax.dot_general(a, b, (((1,), (1,)), ((), ())), preferred_element_type=jnp.float32)


def window(blocks_ref, i, size):
    return pl.ds(pl.multiple_of(blocks_ref[i] * size, size), size)


def early_units(blocks_ref, *refs):
    pieces, (gate_ref, up_ref, gate_out, up_out) = refs[:6], refs[6:]
    eighth = pieces[0].shape[1]
    for weight, out in ((gate_ref, gate_out), (up_ref, up_out)):
        total = None
        for i, piece in enumerate(pieces):
            more = wide(piece[...], weight[:, window(blocks_ref, 4 * (i // 3) + i % 3, eighth)])
            total = more if total is None else total + more
        out[...] = total


def late_units(blocks_ref, mine_ref, theirs_ref, gate_sum, up_sum, gate_ref, up_ref, down_ref, *refs):
    outputs = refs[-8:]
    eighth = mine_ref.shape[1]
    gate, up = gate_sum[...], up_sum[...]
    for i, piece in ((3, mine_ref), (7, theirs_ref)):
        gate = gate + wide(piece[...], gate_ref[:, window(blocks_ref, i, eighth)])
        up = up + wide(piece[...], up_ref[:, window(blocks_ref, i, eighth)])
    act = (gate / (1.0 + jnp.exp(-gate)) * up).astype(jnp.bfloat16)
    for i in (3, 7, 2, 6, 1, 5, 0, 4):
        columns = down_ref[:, window(blocks_ref, i, eighth)]
        outputs[i][...] = jnp.dot(act, columns, preferred_element_type=jnp.float32).astype(jnp.bfloat16)


def turn(mine_x, theirs_x, mine_y, theirs_y, low_ref, high_ref, *refs):
    x_ref, y_ref = refs[-2:]
    split = low_ref.shape[0]
    low, high = slice(0, split), slice(split, x_ref.shape[0])
    for mine, theirs, far, extra, plain, out in (
        (mine_x, theirs_x, low_ref, low, high, x_ref),
        (mine_y, theirs_y, high_ref, high, low, y_ref),
    ):
        out[plain] = (mine[plain].astype(jnp.float32) + theirs[plain].astype(jnp.float32)).astype(jnp.bfloat16)
        total = mine[extra].astype(jnp.float32) + theirs[extra].astype(jnp.float32) + far[...].astype(jnp.float32)
        out[extra] = total.astype(jnp.bfloat16)


def join(mine_ref, theirs_ref, x_ref, y_ref, *refs):
    total = mine_ref[...].astype(jnp.float32) + theirs_ref[...].astype(jnp.float32)
    total = total + x_ref[...].astype(jnp.float32) + y_ref[...].astype(jnp.float32)
    refs[-1][...] = total.astype(jnp.bfloat16)


def held_until(x, *others):
    def kernel(*refs):
        pass

    any_space = pl.BlockSpec(memory_space=pl.ANY)
    return pl.pallas_call(
        kernel,
        out_shape=jax.ShapeDtypeStruct(x.shape, x.dtype),
        in_specs=[any_space] * (1 + len(others)),
        out_specs=any_space,
        input_output_aliases={0: 0},
        name="held_until",
    )(x, *others)


def finish(part_ref, combine_ref, returned_ref, hidden_ref, gain_ref, *refs):
    f32, bf16 = jnp.float32, jnp.bfloat16
    residual_ref, scaled_ref = refs[-2:]
    token_rows = hidden_ref.shape[0]
    eighth = returned_ref.shape[1]
    quarter = 2 * eighth
    squares = jnp.zeros((token_rows, 1), f32)
    for half in range(2):
        start = pl.multiple_of(part_ref[0] * quarter + half * eighth, eighth)
        terms = jnp.dot(combine_ref[half], returned_ref[...], preferred_element_type=f32)
        moe = terms[:token_rows] + terms[token_rows:]
        value = hidden_ref[:, pl.ds(start, eighth)].astype(f32) + moe
        residual_ref[:, half * eighth : (half + 1) * eighth] = value
        scaled_ref[:, half * eighth : (half + 1) * eighth] = (value * gain_ref[:, pl.ds(start, eighth)].astype(f32)).astype(bf16)
        squares = squares + jnp.sum(value * value, axis=1, keepdims=True)
    high = squares.astype(bf16).astype(f32)
    lane = lax.broadcasted_iota(jnp.int32, (token_rows, LANES), 1)
    extra = jnp.where(lane == 0, high, jnp.where(lane == 1, squares - high, 0.0))
    scaled_ref[:, quarter:] = extra.astype(bf16)


def last_step(part_ref, own_ref, core_ref, y_ref, diagonal_ref, weight_ref, query_ref, top_ref, total_ref, mixed_ref, kv_ref, out_ref, *, draft):
    f32, bf16 = jnp.float32, jnp.bfloat16
    token_rows = query_ref.shape[0]
    head_dim = kv_ref.shape[1] // 2
    quarter = own_ref.shape[1] - LANES
    parts = (own_ref, core_ref, y_ref, diagonal_ref)
    squares = jnp.zeros((token_rows, LANES), f32)
    fresh = jnp.zeros((token_rows, 2 * head_dim), f32)
    for i, ref in enumerate(parts):
        rows = pl.ds(pl.multiple_of((part_ref[0] ^ i) * quarter, quarter), quarter)
        fresh = fresh + jnp.dot(ref[:, :quarter], weight_ref[rows, :], preferred_element_type=f32)
        squares = squares + ref[:, quarter:].astype(f32)
    square_sum = jnp.sum(squares, axis=1, keepdims=True)
    fresh = (fresh * inverse_rms(square_sum, len(parts) * quarter)).astype(bf16)
    kv_ref[...] = fresh
    keys = fresh[:, :head_dim]
    values = jnp.concatenate([fresh[:, head_dim:], jnp.ones((token_rows, head_dim), bf16)], axis=1)
    row = lax.broadcasted_iota(jnp.int32, (token_rows, token_rows), 0)
    col = lax.broadcasted_iota(jnp.int32, (token_rows, token_rows), 1)
    seen = (row // draft == col // draft) & (col <= row)
    for h in range(query_ref.shape[1] // head_dim):
        lanes = slice(h * head_dim, (h + 1) * head_dim)
        scores = jnp.where(seen, wide(query_ref[:, lanes], keys) * head_dim ** (-0.5), -jnp.inf)
        top = top_ref[:, lanes]
        new_top = jnp.maximum(top, jnp.max(scores, axis=1, keepdims=True))
        shrink = jnp.exp(top - new_top)
        recent = jnp.dot(jnp.exp(scores - new_top).astype(bf16), values, preferred_element_type=f32)
        denom = shrink * total_ref[:, lanes] + recent[:, head_dim:]
        out_ref[:, lanes] = ((mixed_ref[:, lanes] * shrink + recent[:, :head_dim]) / denom).astype(bf16)


def call(kernel, out_shape, args, smem=0, name=None, away=0, flops=0):
    spaces = [pltpu.SMEM] * smem + [pltpu.VMEM] * (len(args) - smem - away) + [pl.ANY] * away
    out_specs = jax.tree.map(lambda _: pl.BlockSpec(memory_space=pltpu.VMEM), out_shape)
    moved = sum(x.size * x.dtype.itemsize for x in list(args) + jax.tree.leaves(out_shape))
    return pl.pallas_call(
        kernel,
        out_shape=out_shape,
        in_specs=[pl.BlockSpec(memory_space=space) for space in spaces],
        out_specs=out_specs,
        compiler_params=pltpu.CompilerParams(vmem_limit_bytes=48 << 20),
        cost_estimate=pl.CostEstimate(flops=flops, transcendentals=0, bytes_accessed=moved),
        name=name,
    )(*args)


def cached_attention(table_ref, length_ref, query_ref, pool_ref, top_ref, total_ref, mixed_ref, *, max_blocks):
    requests, rows, head_dim = query_ref.shape
    block_len = pool_ref.shape[2]
    span = max_blocks * block_len
    scale = head_dim ** (-0.5)
    places = lax.broadcasted_iota(jnp.int32, (rows, span), 1)
    ones = jnp.ones((span, head_dim), jnp.bfloat16)

    def one(r, carry):
        ids = [table_ref[r * max_blocks + b] for b in range(max_blocks)]
        keys = jnp.concatenate([pool_ref[i, 0] for i in ids], axis=0)
        values = jnp.concatenate([pool_ref[i, 1] for i in ids], axis=0)
        values = jnp.concatenate([values, ones], axis=1)
        scores = lax.dot_general(
            query_ref[r], keys, (((1,), (1,)), ((), ())), preferred_element_type=jnp.float32
        )
        scores = jnp.where(places < length_ref[r], scores * scale, -jnp.inf)
        top = jnp.max(scores, axis=1, keepdims=True)
        exps = jnp.exp(scores - top)
        mixed = jnp.dot(exps.astype(jnp.bfloat16), values, preferred_element_type=jnp.float32)
        top_ref[r] = jnp.broadcast_to(top, (rows, head_dim))
        total_ref[r] = mixed[:, head_dim:]
        mixed_ref[r] = mixed[:, :head_dim]
        return carry

    lax.fori_loop(0, requests, one, 0, unroll=2)


def local(
    hidden_in,
    moe_gain,
    router,
    routes,
    gate_weight,
    up_weight,
    down_weight,
    attn_gain,
    kv_weight,
    queries,
    decode_cache,
    prompt_cache,
    handoff,
    block_table,
    lengths,
):
    peer_count = lax.axis_size("grp")
    expert_count = peer_count // 2
    tp_count = lax.axis_size("tp")
    tp_rank = lax.axis_index("tp")
    token_rows, model_width = hidden_in.shape
    picks_per = routes.shape[1]
    quarter = model_width // tp_count
    capacity = min(token_rows, 3 * token_rows * picks_per // (2 * expert_count))
    total_slots = 2 * expert_count * capacity
    eighth = quarter // 2
    f32, bf16 = jnp.float32, jnp.bfloat16
    shape = jax.ShapeDtypeStruct
    side = lax.axis_index("grp") & 1
    part = tp_rank.astype(jnp.int32).reshape(1)

    packed, slots, scale_in = call(
        functools.partial(prepare, capacity=capacity),
        (shape((peer_count, capacity, eighth), bf16), shape((picks_per, token_rows), jnp.int32), shape((token_rows, LANES), f32)),
        (part, routes.T, hidden_in, moe_gain.reshape(1, model_width)),
        smem=1,
        name="prepare",
    )
    landed = lax.all_to_all(packed, "grp", split_axis=0, concat_axis=0, tiled=True)
    landed = landed.reshape(total_slots, eighth)

    crossed = swapped(prompt_cache[:, 0], "role", 0)
    order = swapped(handoff, "role", 0)

    hidden = hidden_in.astype(f32)
    moe_in = (hidden * scale_in[:, :1] * moe_gain.astype(f32)).astype(bf16)
    logits = jnp.dot(moe_in, router, preferred_element_type=f32)
    gate_probs = jax.nn.softmax(jnp.take_along_axis(logits, routes, axis=1), axis=1)
    targets = jnp.arange(total_slots, dtype=jnp.int32)
    target_slot = targets // (2 * capacity) * capacity + targets % capacity
    hits = (slots.T[:, :, None] == target_slot).astype(f32)
    combine = jnp.sum(hits * gate_probs[:, :, None], axis=1)
    combine_high = combine.astype(bf16)
    combine_low = (combine - combine_high.astype(f32)).astype(bf16)
    both_terms = jnp.concatenate([combine_high, combine_low], axis=0)
    target_half = targets // capacity % 2
    halves = jnp.stack([jnp.where(target_half == i, both_terms, jnp.zeros((), bf16)) for i in range(2)])

    requests, max_blocks = block_table.shape
    head_dim = kv_weight.shape[2]
    flat_weight = kv_weight.reshape(model_width, 2 * head_dim)
    landed = held_until(landed, crossed, order)
    by_y = 2 * total_slots // 3
    from_y = swapped(landed, "tp", 1)
    from_x = held_until(swapped(landed, "grp", 0), from_y)
    mine = (landed, from_x, from_y)
    theirs = tuple(swapped(x, "tp", 0) for x in mine)
    last_mine = swapped(from_x, "tp", 1)
    last_theirs = swapped(last_mine, "tp", 0)

    ordered = held_until(crossed.at[order[0]].get(mode="promise_in_bounds"), from_x)
    arrived = lax.all_to_all(ordered, "grp", split_axis=0, concat_axis=0, tiled=True)

    blocks = jnp.stack(
        [
            (tp_rank ^ (core + 2 * y)) * 2 + (side ^ x)
            for core in range(2)
            for y, x in ((0, 0), (0, 1), (1, 0), (1, 1))
        ]
    ).astype(jnp.int32)
    gate_own, up_own = gate_weight[0].T, up_weight[0].T
    unit_count = gate_own.shape[0]
    sums = call(
        early_units,
        (shape((total_slots, unit_count), f32),) * 2,
        (blocks, *mine, *theirs, gate_own, up_own),
        smem=1,
        name="early_units",
        flops=3 * total_slots * model_width * unit_count,
    )
    sums = call(
        late_units,
        (shape((total_slots, eighth), bf16),) * 8,
        (blocks, last_mine, last_theirs, *sums, gate_own, up_own, down_weight[0], ordered),
        smem=1,
        away=1,
        name="late_units",
        flops=3 * total_slots * model_width * unit_count,
    )

    requests, max_blocks = block_table.shape
    head_dim = kv_weight.shape[2]
    draft_count = token_rows // requests
    per_kv = queries.shape[1] // head_dim
    query_rows = queries.reshape(requests, draft_count * per_kv, head_dim)
    pool = jnp.concatenate([decode_cache[:, 0], arrived], axis=0)
    stats = call(
        functools.partial(cached_attention, max_blocks=max_blocks),
        (shape((requests, draft_count * per_kv, head_dim), f32),) * 3,
        (block_table.reshape(-1), lengths, query_rows, pool),
        smem=2,
        name="cached_attention",
        flops=4 * requests * draft_count * per_kv * head_dim * max_blocks * decode_cache.shape[3],
    )

    draft_count = token_rows // requests
    per_kv = queries.shape[1] // head_dim
    query_rows = queries.reshape(requests, draft_count * per_kv, head_dim)
    pool = jnp.concatenate([decode_cache[:, 0], arrived], axis=0)
    stats = call(
        functools.partial(cached_attention, max_blocks=max_blocks),
        (shape((requests, draft_count * per_kv, head_dim), f32),) * 3,
        (block_table.reshape(-1), lengths, query_rows, pool),
        smem=2,
        name="cached_attention",
        flops=4 * requests * draft_count * per_kv * head_dim * max_blocks * decode_cache.shape[3],
    )

    from_core = tuple(swapped(x, "tp", 0) for x in sums[4:])
    both_ways = (sums[3].astype(f32) + from_core[3].astype(f32)).astype(bf16)
    low, high = swapped(both_ways[:by_y], "tp", 1), swapped(both_ways[by_y:], "grp", 0)
    to_x, to_y = call(
        turn,
        (shape((total_slots, eighth), bf16),) * 2,
        (sums[1], from_core[1], sums[2], from_core[2], low, high, halves, flat_weight),
        away=2,
        name="turn",
    )
    sum_x, sum_y = swapped(to_x, "grp", 0), swapped(to_y, "tp", 1)
    summed = call(
        join,
        shape((total_slots, eighth), bf16),
        (sums[0], from_core[0], sum_x, sum_y, *stats),
        away=3,
        name="join",
    )
    returned = lax.all_to_all(
        summed.reshape(peer_count, capacity, eighth), "grp", split_axis=0, concat_axis=0, tiled=True
    ).reshape(total_slots, eighth)
    stats = tuple(x.reshape(token_rows, per_kv * head_dim) for x in stats)
    residual_out, scaled = call(
        finish,
        (shape((token_rows, quarter), f32), shape((token_rows, quarter + LANES), bf16)),
        (part, halves, returned, hidden_in, attn_gain.reshape(1, model_width), *stats),
        smem=1,
        away=3,
        name="finish",
    )

    scaled_core = swapped(scaled, "tp", 0)
    scaled_y = swapped(scaled, "tp", 1)
    scaled_diagonal = swapped(scaled_y, "tp", 0)
    fresh_kv, attn_out = call(
        functools.partial(last_step, draft=draft_count),
        (shape((token_rows, 2 * head_dim), bf16), shape((token_rows, per_kv * head_dim), bf16)),
        (part, scaled, scaled_core, scaled_y, scaled_diagonal, flat_weight, queries, *stats),
        smem=1,
        name="last_step",
    )
    return (residual_out, fresh_kv.reshape(token_rows, 2, head_dim), attn_out)


def solution(mesh):
    in_specs = (
        P(("role", "grp"), None),
        P(),
        P(),
        P(("role", "grp"), None),
        P("grp", None, "tp"),
        P("grp", None, "tp"),
        P("grp", "tp", None),
        P(),
        P(None, None, "tp"),
        P(("role", "grp"), "tp"),
        P(("role", "grp"), "tp", None, None, None),
        P(("role", "grp"), "tp", None, None, None),
        P(("role", "grp"), None),
        P(("role", "grp"), None),
        P(("role", "grp")),
    )
    out_specs = (P(("role", "grp"), "tp"), P(("role", "grp"), None, "tp"), P(("role", "grp"), "tp"))
    return jax.shard_map(local, mesh=mesh, in_specs=in_specs, out_specs=out_specs, check_vma=False)
```
